32 devices in a mesh: dp: 4 (over x, core), space: 8 (over z, y).
Axes of the slice: x: 2, y: 2, z: 4, core: 2. Of those that a mesh axis runs over, the one named last changes fastest.
Arguments:
- features: bfloat16 [4, 65536, 128], P('dp', 'space'), may hold values from -6 to 6
- child_parent: int32 [4, 65536], P('dp', 'space'), may hold values from 0 to 16383, as said below
- child_code: int32 [4, 65536], P('dp', 'space'), may hold values from 0 to 7
- weight: bfloat16 [8, 128, 128], replicated, may hold values from -0.25 to 0.25
- out_grad: bfloat16 [4, 16384, 128], P('dp', 'space'), may hold values from -6 to 6
Outputs:
- parent_out: bfloat16 [4, 16384, 128], P('dp', 'space')
- feature_grad: bfloat16 [4, 65536, 128], P('dp', 'space')
- weight_grad: float32 [8, 128, 128], replicated
The draws below stay inside these ranges and needn't reach their ends.
Inputs may be any that keep to these rules, and one draw needn't show every extreme that they name: Within one window, child_parent is nondecreasing along the 8192 rows of one device of space. Parent p lies on device p // 2048 of space; at most 2048 rows of one device have their parent on one device, and on every device some device receives exactly 2048. No two fine octants of a window share both parent and child_code.
All inputs are finite; a program needn't handle non-finite values.
Results may differ from the reference program's by a relative error of at most 0.001.
Values may be sent and summed in bfloat16 or wider, within the bound.
No kernel may reach another device: no remote copies, remote signals or barrier semaphores. Data moves between devices by JAX's collectives and lax.ppermute only.
A program may use at most 128 MiB of HBM per device.

```python
import jax
import jax.numpy as jnp
from jax import lax

CIN = 128
COUT = 128
CHILDREN = 8
F_DEV = 8192
PAR_DEV = 2048
FINE = 65536
PARENTS = 16384
WINDOWS = 4
GRAD_ROWS = 262144
N_SPACE = 8


def build_window(key):
    count = N_SPACE
    share = F_DEV // count
    slots = 8 * PAR_DEV
    first, second, third = jax.random.split(key, 3)
    level = jax.random.randint(first, (count, count), 0, share + 1)
    peak = jax.random.randint(second, (count,), 0, count)
    columns = jnp.arange(count)
    level = jnp.where(columns[None, :] == peak[:, None], share, level)
    level = jnp.where(columns[None, :] == ((peak + 1) % count)[:, None], 0, level)
    sent = share + level - jnp.roll(level, -1, axis=1)
    offset = jnp.cumsum(sent, axis=0) - sent
    perms = jax.vmap(lambda sub: jax.random.permutation(sub, slots))(jax.random.split(third, count))
    row_pos = jnp.arange(F_DEV)
    inclusive = jnp.cumsum(sent, axis=1)
    target = jnp.sum(inclusive[:, None, :] <= row_pos[None, :, None], axis=2).astype(jnp.int32)
    start = jnp.take_along_axis(inclusive - sent, target, axis=1)
    place = jnp.take_along_axis(offset, target, axis=1) + row_pos[None, :] - start
    chosen = perms[target, place]
    block = jnp.arange(count)[:, None] * count + target
    keyed = jnp.sort((block * slots + chosen).reshape(-1))
    chosen = keyed % slots
    owner = keyed // slots % count
    parents = owner * PAR_DEV + chosen // 8
    codes = chosen % 8
    return (parents.astype(jnp.int32), codes.astype(jnp.int32))


def build_tree(key):
    base = jax.random.fold_in(key, 7)
    return jax.vmap(build_window)(jax.random.split(base, WINDOWS))


def draw_child_parent(key, part):
    return build_tree(key)[0]


def draw_child_code(key, part):
    return build_tree(key)[1]


def level_of(stream_key, dims, cuts, smallest, high):
    def one(axis_at, parts):
        steps = jax.random.uniform(jax.random.fold_in(jax.random.fold_in(stream_key, 6), axis_at), (parts,), jnp.float32, smallest / len(cuts), high / len(cuts))
        return jnp.repeat(jnp.exp(steps), dims[axis_at] // parts).reshape((-1,) + (1,) * (len(dims) - axis_at - 1))

    gain = one(*cuts[0])
    for cut in cuts[1:]:
        gain = gain * one(*cut)
    return gain


def scatter_about(rng, extent, width, limit, shards=(), dtype=jnp.bfloat16):
    loudness = level_of(rng, extent, shards, -0.22, 0.18) if shards else 1.0
    values = jax.random.normal(rng, extent, jnp.float32) * width * loudness
    return jnp.minimum(jnp.maximum(values, -limit), limit).astype(dtype)


def setup_inputs(seed: int = 0) -> dict:
    keys = jax.random.split(jax.random.key(seed), 6)
    features = scatter_about(keys[0], (WINDOWS, FINE, CIN), 1.0, 6.0, ((0, 4), (1, 8)))
    child_parent = draw_child_parent(jax.random.fold_in(keys[5], 71), 0)
    child_code = draw_child_code(jax.random.fold_in(keys[5], 71), 0)
    weight = scatter_about(keys[3], (CHILDREN, CIN, COUT), (4 * CIN) ** -0.5, 0.25)
    out_grad = scatter_about(keys[4], (WINDOWS, PARENTS, COUT), 1.0, 6.0, ((0, 4), (1, 8)))
    return {"features": features, "child_parent": child_parent, "child_code": child_code, "weight": weight, "out_grad": out_grad}


def reference(features, child_parent, child_code, weight, out_grad):
    weight_flat = weight.reshape(CHILDREN * CIN, COUT)

    def step(packed):
        feats, parents, kinds, grads = packed
        slot_index = parents * CHILDREN + kinds
        grid = jnp.zeros((PARENTS * CHILDREN, CIN), jnp.bfloat16).at[slot_index].set(feats)
        grid = grid.reshape(PARENTS, CHILDREN * CIN)
        result = jnp.dot(grid, weight_flat, preferred_element_type=jnp.float32).astype(jnp.bfloat16)
        parent_grad = jnp.dot(grads, weight_flat.T, preferred_element_type=jnp.float32).astype(jnp.bfloat16)
        parent_grad = parent_grad.reshape(PARENTS * CHILDREN, CIN)
        fine_grad = parent_grad[slot_index]
        term = lax.dot_general(grid, grads, (((0,), (0,)), ((), ())), preferred_element_type=jnp.float32)
        return (result, fine_grad, term)
    parent_out, feature_grad, terms = lax.map(step, (features, child_parent, child_code, out_grad))
    total = lax.optimization_barrier(jnp.sum(terms, axis=0)) / jnp.sqrt(jnp.float32(GRAD_ROWS))
    weight_grad = total.reshape(CHILDREN, CIN, COUT)
    return (parent_out, feature_grad, weight_grad)
```

```python
import jax
import jax.numpy as jnp
from jax import lax
from jax.experimental import pallas as pl
from jax.experimental.pallas import tpu as pltpu
from jax.sharding import PartitionSpec as P

LANES = 128
ALIGN = 16
TILE = 256
META = 32
VMEM_LIMIT = 56 * 1024 * 1024


def column(row):
    return jnp.transpose(jnp.broadcast_to(row.astype(jnp.float32), (LANES, LANES))).astype(jnp.int32)


def pack_kernel(capacity, par_rows, count, dest_ref, parent_ref, code_ref, feats_ref, *rest):
    outs = rest[:count]
    parents, codes, meta, sems, meta_sems = rest[count:]
    lines = parent_ref.shape[0]
    fine_rows = lines * LANES
    tail = meta.shape[1]
    parents[...] = jnp.full(parents.shape, 1 << 20, jnp.int32)
    codes[...] = jnp.zeros(codes.shape, jnp.int32)
    parents[0:lines] = parent_ref[...]
    codes[0:lines] = code_ref[...]
    meta[...] = jnp.zeros(meta.shape, meta.dtype)
    copies = []
    offsets = []
    for m in range(count):
        base = dest_ref[m] * par_rows
        start = jnp.sum((parent_ref[...] < base).astype(jnp.int32))
        offset = jnp.minimum(start // ALIGN * ALIGN, fine_rows - capacity)
        offset = pl.multiple_of(offset, ALIGN)
        offsets.append(offset)
        copy = pltpu.make_async_copy(
            feats_ref.at[pl.ds(offset, capacity)], outs[m].at[pl.ds(0, capacity)], sems.at[m]
        )
        copy.start()
        copies.append(copy)
    lane = lax.broadcasted_iota(jnp.int32, (META, LANES), 1)
    for m in range(count):
        base = dest_ref[m] * par_rows
        line = offsets[m] // LANES
        shift = offsets[m] % LANES

        def window(ref):
            here = pltpu.roll(ref[pl.ds(line, META), :], (LANES - shift) % LANES, 1)
            after = pltpu.roll(ref[pl.ds(line + 1, META), :], (LANES - shift) % LANES, 1)
            return jnp.where(lane < LANES - shift, here, after)

        rel = window(parents) - base
        code = window(codes)
        high = jnp.clip(rel >> 4, -1, 256)
        low = (rel & 15) * 8 + code
        meta[m, 0:META] = high.astype(jnp.float32).astype(jnp.bfloat16)
        meta[m, META : 2 * META] = low.astype(jnp.float32).astype(jnp.bfloat16)
        copy = pltpu.make_async_copy(
            meta.at[m], outs[m].at[pl.ds(capacity, tail)], meta_sems.at[m]
        )
        copy.start()
        copies.append(copy)
    for copy in copies:
        copy.wait()


def pack(dests, parents, codes, feats, capacity, par_rows, total):
    count = dests.shape[0]
    lines = parents.shape[0]
    tail = total - capacity
    return pl.pallas_call(
        lambda *refs: pack_kernel(capacity, par_rows, count, *refs),
        out_shape=[jax.ShapeDtypeStruct((total, LANES), jnp.bfloat16)] * count,
        in_specs=[
            pl.BlockSpec(memory_space=pltpu.SMEM),
            pl.BlockSpec(memory_space=pltpu.VMEM),
            pl.BlockSpec(memory_space=pltpu.VMEM),
            pl.BlockSpec(memory_space=pltpu.VMEM),
        ],
        out_specs=[pl.BlockSpec(memory_space=pl.ANY)] * count,
        scratch_shapes=[
            pltpu.VMEM((lines + META + 8, LANES), jnp.int32),
            pltpu.VMEM((lines + META + 8, LANES), jnp.int32),
            pltpu.VMEM((count, tail, LANES), jnp.bfloat16),
            pltpu.SemaphoreType.DMA((count,)),
            pltpu.SemaphoreType.DMA((count,)),
        ],
        compiler_params=pltpu.CompilerParams(vmem_limit_bytes=VMEM_LIMIT),
        cost_estimate=pl.CostEstimate(flops=0, bytes_accessed=2 * count * total * 256, transcendentals=0),
        name="pack_windows",
    )(dests, parents, codes, feats)


def gather_children_kernel(capacity, par_rows, first, last, payload_ref, weight_ref, *rest):
    if first:
        out_ref, total_ref, hilo_ref = rest
    else:
        prior_ref, out_ref, total_ref, hilo_ref = rest
    total_rows = payload_ref.shape[0]
    lines = total_rows // LANES
    chan_out = weight_ref.shape[1] // 8
    high = payload_ref[capacity : capacity + META, :].astype(jnp.float32).astype(jnp.int32)
    low = payload_ref[capacity + META : capacity + 2 * META, :].astype(jnp.float32).astype(jnp.int32)
    rel = high * 16 + (low >> 3)
    code = low & 7
    tiles = par_rows // TILE
    if first:
        total_ref[...] = jnp.zeros(total_ref.shape, jnp.float32)
    else:
        total_ref[:, 0:chan_out] = prior_ref[...]
        total_ref[:, chan_out : 2 * chan_out] = jnp.zeros(prior_ref.shape, jnp.float32)

    def row_tile(row0, line0, span):
        rows = span * LANES
        feats = payload_ref[row0 : row0 + rows, :]
        products = jnp.dot(feats, weight_ref[...], preferred_element_type=jnp.float32)
        kinds = [column(code[line0 + i : line0 + i + 1, :]) for i in range(span)]
        kind = kinds[0] if span == 1 else jnp.concatenate(kinds, axis=0)
        picked = products[:, 0:chan_out]
        for k in range(1, 8):
            picked = jnp.where(kind == k, products[:, k * chan_out : (k + 1) * chan_out], picked)
        upper = picked.astype(jnp.bfloat16)
        lower = (picked - upper.astype(jnp.float32)).astype(jnp.bfloat16)
        both = jnp.concatenate([upper, lower], axis=1)
        spots = rel[line0 : line0 + span, :]
        valid = (spots >= 0) & (spots < par_rows)
        least = jnp.min(jnp.where(valid, spots, par_rows))
        most = jnp.max(jnp.where(valid, spots, -1))
        spot = jnp.concatenate([spots[i : i + 1, :] for i in range(span)], axis=1)
        rank = lax.broadcasted_iota(jnp.int32, (TILE, rows), 0)

        def body(tile, carry):
            base = pl.multiple_of(tile * TILE, TILE)
            hit = jnp.where(rank == spot - base, 1.0, 0.0).astype(jnp.bfloat16)
            total_ref[pl.ds(base, TILE), :] += jnp.dot(hit, both, preferred_element_type=jnp.float32)
            return carry

        lax.fori_loop(least // TILE, (most + TILE) // TILE, body, 0)

    for t in range(lines // 2):
        row_tile(t * TILE, 2 * t, 2)
    if lines % 2:
        row_tile((lines - 1) * LANES, lines - 1, 1)
    out_ref[...] = (total_ref[:, 0:chan_out] + total_ref[:, chan_out : 2 * chan_out]).astype(out_ref.dtype)


def gather_children(payload, weight_wide, prior, capacity, par_rows, last):
    first = prior is None
    chan_out = weight_wide.shape[1] // 8
    args = (payload, weight_wide) if first else (payload, weight_wide, prior)
    return pl.pallas_call(
        lambda *refs: gather_children_kernel(capacity, par_rows, first, last, *refs),
        out_shape=jax.ShapeDtypeStruct((par_rows, chan_out), jnp.bfloat16 if last else jnp.float32),
        in_specs=[pl.BlockSpec(memory_space=pltpu.VMEM)] * len(args),
        out_specs=pl.BlockSpec(memory_space=pltpu.VMEM),
        scratch_shapes=[
            pltpu.VMEM((par_rows, 2 * chan_out), jnp.float32),
            pltpu.VMEM((8, LANES), jnp.float32),
        ],
        compiler_params=pltpu.CompilerParams(vmem_limit_bytes=VMEM_LIMIT),
        cost_estimate=pl.CostEstimate(flops=0, bytes_accessed=27 << 20, transcendentals=0),
        name="gather_children",
    )(*args)


def backward_kernel(blocks, block_ids_ref, parent_ref, code_ref, feats_ref, weight_ref, *rest):
    cots = rest[:blocks]
    out_ref, kernel_ref, cot_ref, sems = rest[blocks:]
    par_rows, chan_out = cot_ref.shape[1:]
    lines = parent_ref.shape[0]
    copies = [
        pltpu.make_async_copy(cots[i], cot_ref.at[block_ids_ref[i]], sems.at[i]) for i in range(blocks)
    ]
    for copy in copies:
        copy.start()
    kernel_ref[...] = jnp.zeros(kernel_ref.shape, jnp.float32)
    for copy in copies:
        copy.wait()
    rank = lax.broadcasted_iota(jnp.int32, (LANES, TILE), 1)

    def row_tile(t, carry):
        lines_here = parent_ref[pl.ds(2 * t, 2), :]
        codes_here = code_ref[pl.ds(2 * t, 2), :]
        least = jnp.min(lines_here[0:1, :])
        most = jnp.max(lines_here[1:2, :])
        spots = [column(lines_here[i : i + 1, :]) for i in range(2)]
        kind = jnp.concatenate([column(codes_here[i : i + 1, :]) for i in range(2)], axis=0)
        wide = [jnp.concatenate([s, s], axis=1) for s in spots]

        def body(tile, rows):
            base = tile * TILE
            hit = jnp.concatenate(
                [jnp.where(rank + base == w, 1.0, 0.0).astype(jnp.bfloat16) for w in wide], axis=0
            )
            block = base // par_rows
            inner = pl.multiple_of(base % par_rows, TILE)
            return rows + jnp.dot(hit, cot_ref[block, pl.ds(inner, TILE), :], preferred_element_type=jnp.float32)

        rows = lax.fori_loop(
            least // TILE, most // TILE + 1, body, jnp.zeros((TILE, chan_out), jnp.float32)
        )
        spread = jnp.concatenate(
            [jnp.where(kind == k, rows, 0.0).astype(jnp.bfloat16) for k in range(8)], axis=1
        )
        here = pl.multiple_of(t * TILE, TILE)
        out_ref[pl.ds(here, TILE), :] = jnp.dot(
            spread, weight_ref[...], preferred_element_type=jnp.float32
        ).astype(out_ref.dtype)
        kernel_ref[...] += lax.dot_general(
            feats_ref[pl.ds(here, TILE), :],
            spread,
            (((0,), (0,)), ((), ())),
            preferred_element_type=jnp.float32,
        )
        return carry

    lax.fori_loop(0, lines // 2, row_tile, 0)


def backward(block_ids, parents, codes, feats, weight_tall, cots):
    blocks = len(cots)
    par_rows, chan_out = cots[0].shape
    chan_in = feats.shape[1]
    vmem = pl.BlockSpec(memory_space=pltpu.VMEM)
    return pl.pallas_call(
        lambda *refs: backward_kernel(blocks, *refs),
        out_shape=[
            jax.ShapeDtypeStruct(feats.shape, jnp.bfloat16),
            jax.ShapeDtypeStruct((chan_in, 8 * chan_out), jnp.float32),
        ],
        in_specs=[pl.BlockSpec(memory_space=pltpu.SMEM), vmem, vmem, vmem, vmem]
        + [pl.BlockSpec(memory_space=pl.ANY)] * blocks,
        out_specs=[vmem, vmem],
        scratch_shapes=[
            pltpu.VMEM((blocks, par_rows, chan_out), jnp.bfloat16),
            pltpu.SemaphoreType.DMA((blocks,)),
        ],
        compiler_params=pltpu.CompilerParams(vmem_limit_bytes=VMEM_LIMIT),
        cost_estimate=pl.CostEstimate(flops=0, bytes_accessed=150 << 20, transcendentals=0),
        name="fine_gradients",
    )(block_ids, parents, codes, feats, weight_tall, *cots)


def reduce_kernel_terms(terms):
    rows = terms.shape[0]
    parts = lax.axis_size("dp") * lax.axis_size("space")
    axes = ("dp", "space")
    pieces = lax.all_to_all(
        terms.reshape(parts, rows // parts, terms.shape[1]), axes, 0, 0, tiled=True
    )
    mine = jnp.sum(pieces, axis=0)
    back = lax.all_to_all(
        jnp.broadcast_to(mine[None], (parts,) + mine.shape), axes, 0, 0, tiled=True
    )
    return back.reshape(terms.shape)


def cycle_of(size):
    return list(range(0, size, 2)) + list(range(size - 1, 0, -2))


def collect_blocks(block, space_size):
    cycle = cycle_of(space_size)
    place = {d: i for i, d in enumerate(cycle)}
    me = lax.axis_index("space")
    spot = jnp.asarray([place[d] for d in range(space_size)], jnp.int32)[me]
    ring = jnp.asarray(cycle, jnp.int32)
    ahead = [(cycle[i], cycle[(i + 1) % space_size]) for i in range(space_size)]
    behind = [(b, a) for a, b in ahead]
    blocks, ids = [block], [me]
    right = left = block
    for step in range(1, space_size // 2 + 1):
        right = lax.ppermute(right, "space", ahead)
        blocks.append(right)
        ids.append(ring[(spot - step) % space_size])
        if step < space_size // 2:
            left = lax.ppermute(left, "space", behind)
            blocks.append(left)
            ids.append(ring[(spot + step) % space_size])
    return blocks, jnp.stack(ids).astype(jnp.int32)


def per_device(features, child_parent, child_code, weight, out_grad):
    fine_rows = features[0]
    row_count = fine_rows.shape[0]
    parents = child_parent[0].reshape(row_count // LANES, LANES)
    codes = child_code[0].reshape(row_count // LANES, LANES)
    cotangent = out_grad[0]
    par_rows = cotangent.shape[0]
    kinds_total, chan_in, chan_out = weight.shape
    space_size = lax.axis_size("space")
    me = lax.axis_index("space")
    capacity = 2 * row_count // space_size + ALIGN
    total = -(-(capacity + 2 * META) // LANES) * LANES
    weight_wide = jnp.transpose(weight, (1, 0, 2)).reshape(chan_in, kinds_total * chan_out)
    weight_tall = jnp.transpose(weight, (0, 2, 1)).reshape(kinds_total * chan_out, chan_in)
    dests = (me ^ jnp.arange(space_size)).astype(jnp.int32)

    payloads = pack(dests, parents, codes, fine_rows, capacity, par_rows, total)
    cotangent, *payloads = lax.optimization_barrier((cotangent, *payloads))
    blocks, ids = collect_blocks(cotangent, space_size)
    arrived = [
        lax.ppermute(payloads[m], "space", [(i, i ^ m) for i in range(space_size)])
        for m in range(1, space_size)
    ]
    feature_grad, term = backward(ids, parents, codes, fine_rows, weight_tall, blocks)
    summed = reduce_kernel_terms(term.reshape(chan_in * kinds_total, chan_out))
    acc = gather_children(payloads[0], weight_wide, None, capacity, par_rows, False)
    for m in range(1, space_size):
        acc = gather_children(
            arrived[m - 1], weight_wide, acc, capacity, par_rows, m == space_size - 1
        )
    total_rows = row_count * space_size * lax.axis_size("dp")
    weight_grad = summed.reshape(chan_in, kinds_total, chan_out).transpose(1, 0, 2) / jnp.sqrt(
        jnp.float32(total_rows)
    )
    return (acc[None], feature_grad[None], weight_grad)


def solution(mesh):
    placed = (
        P("dp", "space", None),
        P("dp", "space"),
        P("dp", "space"),
        P(),
        P("dp", "space", None),
    )
    return jax.shard_map(
        per_device,
        mesh=mesh,
        in_specs=placed,
        out_specs=(P("dp", "space", None), P("dp", "space", None), P()),
        check_vma=False,
    )
```

```python
import jax
import jax.numpy as jnp
from jax import lax
from jax.experimental import pallas as pl
from jax.experimental.pallas import tpu as pltpu
from jax.sharding import PartitionSpec as P

LANES = 128
ALIGN = 16
TILE = 256
VMEM_LIMIT = 60 * 1024 * 1024


def column(row):
    return jnp.transpose(jnp.broadcast_to(row.astype(jnp.float32), (LANES, LANES))).astype(jnp.int32)


def pack_kernel(half, par_rows, parent_ref, code_ref, feats_ref, early_ref, late_ref, wide, parents, codes, stage_ref, sems):
    lines = parent_ref.shape[0]
    count = early_ref.shape[0]
    fine_rows = lines * LANES
    half_lines = half // LANES
    parents[...] = jnp.full(parents.shape, 1 << 20, jnp.int32)
    codes[...] = jnp.zeros(codes.shape, jnp.int32)
    parents[0:lines] = parent_ref[...]
    codes[0:lines] = code_ref[...]
    wide[0:fine_rows] = feats_ref[...].astype(jnp.float32)
    wide[fine_rows:] = jnp.zeros((wide.shape[0] - fine_rows, wide.shape[1]), jnp.float32)
    lane = lax.broadcasted_iota(jnp.int32, (8, LANES), 1)
    copies = []
    for m in range(count):
        base = m * par_rows
        start = jnp.sum((parent_ref[...] < base).astype(jnp.int32))
        for part, out in enumerate((early_ref, late_ref)):
            here = start + part * half
            line = here // LANES
            shift = here % LANES

            def window(ref):
                now = pltpu.roll(ref[pl.ds(line, 8), :], (LANES - shift) % LANES, 1)
                after = pltpu.roll(ref[pl.ds(line + 1, 8), :], (LANES - shift) % LANES, 1)
                return jnp.where(lane < LANES - shift, now, after)

            rel = window(parents) - base
            high = jnp.clip(rel >> 4, -1, 256)
            low = (rel & 15) * 8 + window(codes)
            both = jnp.concatenate([high, low], axis=0).astype(jnp.float32)
            stage_ref[m, part, 0:half] = wide[pl.ds(here, half), :].astype(jnp.bfloat16)
            stage_ref[m, part, half : half + ALIGN] = both.astype(jnp.bfloat16)
            copy = pltpu.make_async_copy(stage_ref.at[m, part], out.at[m], sems.at[m, part])
            copy.start()
            copies.append(copy)
    for copy in copies:
        copy.wait()


def pack(parents, codes, feats, count, half, par_rows):
    lines = parents.shape[0]
    rows = half + ALIGN
    vmem = pl.BlockSpec(memory_space=pltpu.VMEM)
    return pl.pallas_call(
        lambda *refs: pack_kernel(half, par_rows, *refs),
        out_shape=[jax.ShapeDtypeStruct((count, rows, LANES), jnp.bfloat16)] * 2,
        in_specs=[vmem] * 3,
        out_specs=[pl.BlockSpec(memory_space=pl.ANY)] * 2,
        scratch_shapes=[
            pltpu.VMEM((feats.shape[0] + 2 * half + 8, LANES), jnp.float32),
            pltpu.VMEM((lines + half // LANES + 16, LANES), jnp.int32),
            pltpu.VMEM((lines + half // LANES + 16, LANES), jnp.int32),
            pltpu.VMEM((count, 2, rows, LANES), jnp.bfloat16),
            pltpu.SemaphoreType.DMA((count, 2)),
        ],
        compiler_params=pltpu.CompilerParams(vmem_limit_bytes=VMEM_LIMIT),
        name="pack_windows",
    )(parents, codes, feats)


def spread_kinds(kind, rows, kinds_total):
    zero = jnp.zeros((), rows.dtype)
    tag = kind.astype(jnp.float32).astype(rows.dtype)
    return jnp.concatenate(
        [jnp.where(tag == jnp.asarray(k, rows.dtype), rows, zero) for k in range(kinds_total)], axis=1
    )


def place_children_kernel(half, first, payload_ref, weight_ref, *rest):
    if first:
        out_ref, total_ref, rel_ref, code_ref, ends_vmem, ends_ref, sem = rest
    else:
        prior_ref, out_ref, total_ref, rel_ref, code_ref, ends_vmem, ends_ref, sem = rest
    par_rows, chan_out = out_ref.shape
    sources = payload_ref.shape[0]
    kinds_total = weight_ref.shape[0] // payload_ref.shape[2]
    lines = half // LANES
    size = min(2 * TILE, half)
    parts = size // TILE
    per = TILE // LANES
    window = min(5 * TILE // 2, par_rows)
    meta = payload_ref[:, half : half + ALIGN, :].astype(jnp.float32).astype(jnp.int32)
    rel = meta[:, 0:8] * 16 + (meta[:, 8:16] >> 3)
    line = lax.broadcasted_iota(jnp.int32, rel.shape, 1)
    rel = jnp.where(line < lines, rel, par_rows).reshape(8 * sources, LANES)
    rel_ref[...] = rel
    code_ref[...] = (meta[:, 8:16] & 7).reshape(8 * sources, LANES)
    least = jnp.min(jnp.maximum(rel, 0), axis=1, keepdims=True)
    most = jnp.max(jnp.where(rel < par_rows, rel, -1), axis=1, keepdims=True)
    ends_vmem[0] = jnp.broadcast_to(least, rel.shape)
    ends_vmem[1] = jnp.broadcast_to(most, rel.shape)
    copy = pltpu.make_async_copy(ends_vmem, ends_ref, sem)
    copy.start()
    total_ref[...] = jnp.zeros(total_ref.shape, jnp.float32)
    if not first:
        total_ref[:, 0:chan_out] = prior_ref[...]
    copy.wait()
    chunks = half // size

    def chunk(step, carry):
        s = step // chunks
        c = step % chunks
        line0 = 8 * s + c * (size // LANES)
        mosts = [
            jnp.maximum(ends_ref[1, line0 + per * p, 0], ends_ref[1, line0 + per * p + per - 1, 0])
            for p in range(parts)
        ]
        starts = [
            pl.multiple_of(jnp.minimum(ends_ref[0, line0 + per * p, 0] // 8 * 8, par_rows - window), 8)
            for p in range(parts)
        ]
        slow = mosts[0] >= starts[0] + window
        live = mosts[0] >= 0
        for p in range(1, parts):
            slow = slow | (mosts[p] >= starts[p] + window)
            live = live | (mosts[p] >= 0)

        def work(extra):
            feats = payload_ref[s, pl.ds(pl.multiple_of(c * size, size), size), :]
            kinds = [column(code_ref[pl.ds(line0 + i, 1), :]) for i in range(size // LANES)]
            spread = spread_kinds(jnp.concatenate(kinds, axis=0), feats, kinds_total)
            product = jnp.dot(spread, weight_ref[...], preferred_element_type=jnp.float32)
            upper = product.astype(jnp.bfloat16)
            lower = (product - upper.astype(jnp.float32)).astype(jnp.bfloat16)
            both = jnp.concatenate([upper, lower], axis=1)
            for p in range(parts):
                count = TILE // LANES
                spots = [rel_ref[pl.ds(line0 + p * count + i, 1), :] for i in range(count)]
                spot = jnp.concatenate(spots, axis=1)
                mine = both[p * TILE : (p + 1) * TILE]

                def add(start, width, floor):
                    rank = lax.broadcasted_iota(jnp.int32, (width, TILE), 0) + start
                    hit = rank == spot
                    if floor is not None:
                        hit = hit & (rank >= floor)
                    total_ref[pl.ds(start, width), :] += jnp.dot(
                        jnp.where(hit, 1.0, 0.0).astype(jnp.bfloat16),
                        mine,
                        preferred_element_type=jnp.float32,
                    )

                add(starts[p], window, None)
                if extra:

                    def body(i, carry):
                        floor = starts[p] + window + i * TILE
                        add(pl.multiple_of(jnp.minimum(floor, par_rows - TILE), 8), TILE, floor)
                        return carry

                    lax.fori_loop(0, (mosts[p] + TILE - starts[p] - window) // TILE, body, 0)

        pl.when(live & slow)(lambda: work(True))
        pl.when(live & jnp.logical_not(slow))(lambda: work(False))
        return carry

    lax.fori_loop(0, sources * chunks, chunk, 0)
    out_ref[...] = (total_ref[:, 0:chan_out] + total_ref[:, chan_out : 2 * chan_out]).astype(out_ref.dtype)


def place_children(payload, weight_flat, prior, par_rows, last):
    first = prior is None
    chan_out = weight_flat.shape[1]
    sources = payload.shape[0]
    args = (payload, weight_flat) if first else (payload, weight_flat, prior)
    return pl.pallas_call(
        lambda *refs: place_children_kernel(payload.shape[1] - ALIGN, first, *refs),
        out_shape=jax.ShapeDtypeStruct((par_rows, chan_out), jnp.bfloat16 if last else jnp.float32),
        in_specs=[pl.BlockSpec(memory_space=pltpu.VMEM)] * len(args),
        out_specs=pl.BlockSpec(memory_space=pltpu.VMEM),
        scratch_shapes=[
            pltpu.VMEM((par_rows, 2 * chan_out), jnp.float32),
            pltpu.VMEM((8 * sources, LANES), jnp.int32),
            pltpu.VMEM((8 * sources, LANES), jnp.int32),
            pltpu.VMEM((2, 8 * sources, LANES), jnp.int32),
            pltpu.SMEM((2, 8 * sources, LANES), jnp.int32),
            pltpu.SemaphoreType.DMA(()),
        ],
        compiler_params=pltpu.CompilerParams(vmem_limit_bytes=VMEM_LIMIT),
        name="place_children",
    )(*args)


def stage_kernel(blocks, priors, shares, offset, table_ref, ends_ref, parent_ref, code_ref, feats_ref, weight_ref, *rest):
    cots = rest[:blocks]
    prior_refs = rest[blocks : blocks + priors]
    outs = rest[blocks + priors : 2 * blocks + priors]
    rest = rest[2 * blocks + priors :]
    terms_ref = rest[-1]
    kinds_total, chan_in, chan_out = terms_ref.shape
    size = 2 * TILE
    lines = size // LANES
    if priors:
        total = prior_refs[0][...]
        for prior_ref in prior_refs[1:]:
            total = total + prior_ref[...]
        terms_ref[...] = total
    else:
        terms_ref[...] = jnp.zeros(terms_ref.shape, jnp.float32)
    parents = parent_ref[...]
    for i, cot_ref in enumerate(cots):
        base = table_ref[offset + i]
        span = cot_ref.shape[0]
        window = min(3 * TILE, span)
        first = jnp.sum((parents < base).astype(jnp.int32)) // size
        last = (jnp.sum((parents < base + span).astype(jnp.int32)) + size - 1) // size

        def chunk(c, carry):
            starts, mosts = [], []
            for part in range(2):
                least = jnp.clip(ends_ref[0, 2 * c + part] - base, 0, span - 1)
                mosts.append(jnp.minimum(ends_ref[1, 2 * c + part] - base, span - 1))
                starts.append(pl.multiple_of(jnp.minimum(least // 16 * 16, span - window), 16))
            slow = (mosts[0] >= starts[0] + window) | (mosts[1] >= starts[1] + window)

            def work(extra):
                slots = (parent_ref[pl.ds(c * lines, lines), :] - base) * 8 + code_ref[
                    pl.ds(c * lines, lines), :
                ]
                slot = [column(slots[j : j + 1, :]) for j in range(lines)]
                kind = jnp.concatenate(slot, axis=0) & 7
                picked = []
                for part in range(2):
                    spot = jnp.concatenate(slot[2 * part : 2 * part + 2], axis=0) >> 3

                    def pull(start, width, floor):
                        lane = lax.broadcasted_iota(jnp.int32, (TILE, LANES), 1) + start
                        hits = []
                        for off in range(0, width, LANES):
                            hit = lane + off == spot
                            if floor is not None:
                                hit = hit & (lane + off >= floor)
                            hits.append(jnp.where(hit, 1.0, 0.0).astype(jnp.bfloat16))
                        return jnp.dot(
                            jnp.concatenate(hits, axis=1),
                            cot_ref[pl.ds(start, width), :],
                            preferred_element_type=jnp.float32,
                        )

                    rows = pull(starts[part], window, None)
                    if extra:

                        def body(n, rows):
                            floor = starts[part] + window + n * TILE
                            at = pl.multiple_of(jnp.minimum(floor, span - TILE), 16)
                            return rows + pull(at, TILE, floor)

                        count = (mosts[part] + TILE - starts[part] - window) // TILE
                        rows = lax.fori_loop(0, count, body, rows)
                    picked.append(rows.astype(jnp.bfloat16))
                spread = spread_kinds(kind, jnp.concatenate(picked, axis=0), kinds_total)
                there = pl.ds(pl.multiple_of((c - first) * size, size), size)
                outs[i][there, :] = jnp.dot(
                    spread, weight_ref[...], preferred_element_type=jnp.float32
                ).astype(jnp.bfloat16)
                part = lax.dot_general(
                    feats_ref[pl.ds(pl.multiple_of(c * size, size), size), :],
                    spread,
                    (((0,), (0,)), ((), ())),
                    preferred_element_type=jnp.float32,
                )
                for k in range(kinds_total):
                    terms_ref[k] += part[:, k * chan_out : (k + 1) * chan_out]

            pl.when(slow)(lambda: work(True))
            pl.when(jnp.logical_not(slow))(lambda: work(False))
            return carry

        lax.fori_loop(first, last, chunk, 0)
    if shares:
        per = kinds_total // shares
        for m in range(shares):
            owner = table_ref[offset + blocks + m]
            rest[m][...] = terms_ref[pl.ds(owner * per, per)].reshape(rest[m].shape)


def stage(table, offset, ends, parents, codes, feats, weight_tall, cots, priors, shares, rows):
    blocks = len(cots)
    chan_out = cots[0].shape[1]
    chan_in = feats.shape[1]
    kinds_total = weight_tall.shape[0] // chan_out
    smem = pl.BlockSpec(memory_space=pltpu.SMEM)
    vmem = pl.BlockSpec(memory_space=pltpu.VMEM)
    args = (table, ends, parents, codes, feats, weight_tall, *cots, *priors)
    outs = [jax.ShapeDtypeStruct((rows, chan_in), jnp.bfloat16)] * blocks
    scratch = []
    terms_shape = (kinds_total, chan_in, chan_out)
    if shares:
        outs += [jax.ShapeDtypeStruct((kinds_total * chan_in // shares, chan_out), jnp.float32)] * shares
        scratch = [pltpu.VMEM(terms_shape, jnp.float32)]
    else:
        outs += [jax.ShapeDtypeStruct(terms_shape, jnp.float32)]
    return pl.pallas_call(
        lambda *refs: stage_kernel(blocks, len(priors), shares, offset, *refs),
        out_shape=outs,
        in_specs=[smem, smem] + [vmem] * (len(args) - 2),
        out_specs=[vmem] * len(outs),
        scratch_shapes=scratch,
        compiler_params=pltpu.CompilerParams(vmem_limit_bytes=VMEM_LIMIT),
        name="fine_gradients",
    )(*args)


def merge_kernel(spans, offset, table_ref, parent_ref, *rest):
    out_ref = rest[-1]
    size = 2 * TILE
    out_ref[...] = jnp.zeros(out_ref.shape, out_ref.dtype)
    parents = parent_ref[...]
    for i, span in enumerate(spans):
        base = table_ref[offset + i]
        first = jnp.sum((parents < base).astype(jnp.int32)) // size
        last = (jnp.sum((parents < base + span).astype(jnp.int32)) + size - 1) // size

        def chunk(c, carry):
            here = pl.ds(pl.multiple_of(c * size, size), size)
            there = pl.ds(pl.multiple_of((c - first) * size, size), size)
            out_ref[here, :] = (
                out_ref[here, :].astype(jnp.float32) + rest[i][there, :].astype(jnp.float32)
            ).astype(out_ref.dtype)
            return carry

        lax.fori_loop(first, last, chunk, 0)


def merge(table, offset, parents, spans, parts, shape):
    vmem = pl.BlockSpec(memory_space=pltpu.VMEM)
    return pl.pallas_call(
        lambda *refs: merge_kernel(spans, offset, *refs),
        out_shape=jax.ShapeDtypeStruct(shape, jnp.bfloat16),
        in_specs=[pl.BlockSpec(memory_space=pltpu.SMEM)] + [vmem] * (1 + len(parts)),
        out_specs=vmem,
        compiler_params=pltpu.CompilerParams(vmem_limit_bytes=VMEM_LIMIT),
        name="merge_gradients",
    )(table, parents, *parts)

GATE_EARLY = 3


def after(value, *marks):
    return lax.optimization_barrier((value, *marks))[0]


def swap(value, mask, axis):
    size = lax.axis_size(axis)
    return lax.ppermute(value, axis, [(i, i ^ mask) for i in range(size)])


def pick(parts, index):
    return lax.dynamic_index_in_dim(parts, index, 0, keepdims=False)


def sum_terms(keep, send, mark):
    space_size = lax.axis_size("space")
    dp_size = lax.axis_size("dp")
    total = keep + swap(send, 1, "dp")
    trail = [("dp", 1)]
    steps = [("dp", 1 << b) for b in range(1, dp_size.bit_length() - 1)] + [("space", 1)]
    for axis, bit in steps:
        total = mark(("down", axis, bit), total)
        mine = lax.axis_index(axis) // bit % 2
        parts = total.reshape(2, total.shape[0] // 2, total.shape[1])
        total = pick(parts, mine) + swap(pick(parts, 1 - mine), bit, axis)
        trail.append((axis, bit))
    total = mark("across", total)
    if space_size == 8:
        total = (total + swap(total, 2, "space")) + (swap(total, 4, "space") + swap(total, 6, "space"))
    else:
        bit = 2
        while bit < space_size:
            total = total + swap(total, bit, "space")
            bit *= 2
    spot = lax.axis_index("dp") // 2 * 2 + lax.axis_index("space") % 2
    if dp_size == 4:
        total = mark("up", total)
        pairs = [(d * space_size + s, (d ^ 2) * space_size + (s ^ 1)) for d in range(4) for s in range(space_size)]
        by = [total, swap(total, 1, "space"), swap(total, 2, "dp"), lax.ppermute(total, ("dp", "space"), pairs)]
        wide = []
        for place in range(4):
            piece = by[0]
            for k in range(1, 4):
                piece = jnp.where(spot ^ k == place, by[k], piece)
            wide.append(piece)
        total = jnp.concatenate(wide, axis=0)
        trail = trail[:1]
    for axis, bit in trail[::-1]:
        total = mark(("up", axis, bit), total)
        mine = lax.axis_index(axis) // bit % 2
        other = swap(total, bit, axis)
        total = jnp.where(
            mine == 0, jnp.concatenate([total, other]), jnp.concatenate([other, total])
        )
    return total


def table_row(place, bit, cycle, par_rows):
    size = len(cycle)
    spot = cycle.index(place)
    row = [place * par_rows]
    for step in range(1, size // 2):
        row += [cycle[(spot - step) % size] * par_rows, cycle[(spot + step) % size] * par_rows]
    far = cycle[(spot + size // 2) % size] * par_rows
    return row + [far, far + par_rows // 2, bit, 1 - bit]


def per_device(features, child_parent, child_code, weight, out_grad):
    fine_rows = features[0]
    row_count = fine_rows.shape[0]
    parents = child_parent[0].reshape(row_count // LANES, LANES)
    codes = child_code[0].reshape(row_count // LANES, LANES)
    cotangent = out_grad[0]
    par_rows = cotangent.shape[0]
    kinds_total, chan_in, chan_out = weight.shape
    space_size = lax.axis_size("space")
    dp_size = lax.axis_size("dp")
    me = lax.axis_index("space")
    capacity = 2 * row_count // space_size
    weight_flat = weight.reshape(kinds_total * chan_in, chan_out)
    weight_tall = jnp.transpose(weight, (0, 2, 1)).reshape(kinds_total * chan_out, chan_in)
    steps = space_size // 2
    half = par_rows // 2
    cycle = list(range(0, space_size, 2)) + list(range(space_size - 1, 0, -2))
    ahead = [(cycle[i], cycle[(i + 1) % space_size]) for i in range(space_size)]
    behind = [(b, a) for a, b in ahead]
    dp_bit = lax.axis_index("dp") % 2
    table = jnp.asarray(
        [table_row(d, b, cycle, par_rows) for d in range(space_size) for b in range(2)], jnp.int32
    )
    table = lax.dynamic_index_in_dim(table, 2 * me + dp_bit, 0, keepdims=False)
    early, late = pack(parents, codes, fine_rows, space_size, capacity // 2, par_rows)

    tiles = child_parent[0].reshape(row_count // TILE, TILE)
    ends = jnp.stack([tiles[:, 0], tiles[:, TILE - 1]])
    size = 2 * TILE
    window_rows = (-(-(2 * row_count // space_size) // size) + 1) * size
    grads, spans, terms_parts = [], [], []

    def advance(step, blocks, shares=0):
        *parts, = stage(
            table, max(2 * step - 1, 0), ends, parents, codes, fine_rows, weight_tall, blocks,
            terms_parts if shares else (), shares, window_rows,
        )
        grads.extend(parts[: len(blocks)])
        spans.extend(block.shape[0] for block in blocks)
        return parts[len(blocks) :]

    def exchange(windows, mark):
        return lax.all_to_all(after(windows, mark), "space", 0, 0, tiled=True)

    right = left = cotangent
    blocks = (cotangent,)
    for step in range(1, steps + 1):
        if step == steps:
            right, left = right[:half], left[half:]
        right = lax.ppermute(right, "space", ahead)
        left = lax.ppermute(left, "space", behind)
        terms_parts += advance(step - 1, blocks)
        blocks = (right, left)
        if step < steps:
            right, left = lax.optimization_barrier((right, left, terms_parts[-1]))[:2]
        if step == GATE_EARLY:
            early = exchange(early, right)
    blocks = (blocks[0], after(blocks[1], terms_parts[-1]))
    keep, give = advance(steps, blocks, 2)
    late = lax.all_to_all(after(late, *blocks), "space", 0, 0, tiled=True)
    placed = place_children(after(early, keep), weight_flat, None, par_rows, False)
    acc = place_children(late, weight_flat, placed, par_rows, True)

    feature_grad = merge(table, 0, parents, spans, grads, fine_rows.shape)

    def mark(name, value):
        if name == ("down", "dp", 2):
            return after(value, placed)
        if name == ("up", "dp", 1):
            return after(value, acc)
        return after(value, feature_grad) if name == "across" else value

    terms = sum_terms(keep, give, mark)
    total_rows = row_count * space_size * dp_size
    summed = terms.reshape(kinds_total, chan_in, chan_out)
    weight_grad = summed / jnp.sqrt(jnp.float32(total_rows))
    return (acc[None], feature_grad[None], weight_grad)


def solution(mesh):
    placed = (
        P("dp", "space", None),
        P("dp", "space"),
        P("dp", "space"),
        P(),
        P("dp", "space", None),
    )
    return jax.shard_map(
        per_device,
        mesh=mesh,
        in_specs=placed,
        out_specs=(P("dp", "space", None), P("dp", "space", None), P()),
        check_vma=False,
    )
```

```python
import jax
import jax.numpy as jnp
from jax import lax
from jax.experimental import pallas as pl
from jax.experimental.pallas import tpu as pltpu
from jax.sharding import PartitionSpec as P

LANES = 128
ALIGN = 16
TILE = 256
VMEM_LIMIT = 60 * 1024 * 1024


def column(row):
    return jnp.transpose(jnp.broadcast_to(row.astype(jnp.float32), (LANES, LANES))).astype(jnp.int32)


def pack_kernel(half, par_rows, parent_ref, code_ref, feats_ref, early_ref, late_ref, wide, parents, codes, stage_ref, sems):
    lines = parent_ref.shape[0]
    count = early_ref.shape[0]
    fine_rows = lines * LANES
    half_lines = half // LANES
    parents[...] = jnp.full(parents.shape, 1 << 20, jnp.int32)
    codes[...] = jnp.zeros(codes.shape, jnp.int32)
    parents[0:lines] = parent_ref[...]
    codes[0:lines] = code_ref[...]
    wide[0:fine_rows] = feats_ref[...].astype(jnp.float32)
    wide[fine_rows:] = jnp.zeros((wide.shape[0] - fine_rows, wide.shape[1]), jnp.float32)
    lane = lax.broadcasted_iota(jnp.int32, (8, LANES), 1)
    copies = []
    for m in range(count):
        base = m * par_rows
        start = jnp.sum((parent_ref[...] < base).astype(jnp.int32))
        for part, out in enumerate((early_ref, late_ref)):
            here = start + part * half
            line = here // LANES
            shift = here % LANES

            def window(ref):
                now = pltpu.roll(ref[pl.ds(line, 8), :], (LANES - shift) % LANES, 1)
                after = pltpu.roll(ref[pl.ds(line + 1, 8), :], (LANES - shift) % LANES, 1)
                return jnp.where(lane < LANES - shift, now, after)

            rel = window(parents) - base
            high = jnp.clip(rel >> 4, -1, 256)
            low = (rel & 15) * 8 + window(codes)
            both = jnp.concatenate([high, low], axis=0).astype(jnp.float32)
            stage_ref[m, part, 0:half] = wide[pl.ds(here, half), :].astype(jnp.bfloat16)
            stage_ref[m, part, half : half + ALIGN] = both.astype(jnp.bfloat16)
            copy = pltpu.make_async_copy(stage_ref.at[m, part], out.at[m], sems.at[m, part])
            copy.start()
            copies.append(copy)
    for copy in copies:
        copy.wait()


def pack(parents, codes, feats, count, half, par_rows):
    lines = parents.shape[0]
    rows = half + ALIGN
    vmem = pl.BlockSpec(memory_space=pltpu.VMEM)
    return pl.pallas_call(
        lambda *refs: pack_kernel(half, par_rows, *refs),
        out_shape=[jax.ShapeDtypeStruct((count, rows, LANES), jnp.bfloat16)] * 2,
        in_specs=[vmem] * 3,
        out_specs=[pl.BlockSpec(memory_space=pl.ANY)] * 2,
        scratch_shapes=[
            pltpu.VMEM((feats.shape[0] + 2 * half + 8, LANES), jnp.float32),
            pltpu.VMEM((lines + half // LANES + 16, LANES), jnp.int32),
            pltpu.VMEM((lines + half // LANES + 16, LANES), jnp.int32),
            pltpu.VMEM((count, 2, rows, LANES), jnp.bfloat16),
            pltpu.SemaphoreType.DMA((count, 2)),
        ],
        compiler_params=pltpu.CompilerParams(vmem_limit_bytes=VMEM_LIMIT),
        name="pack_windows",
    )(parents, codes, feats)


def spread_kinds(kind, rows, kinds_total):
    zero = jnp.zeros((), rows.dtype)
    tag = kind.astype(jnp.float32).astype(rows.dtype)
    return jnp.concatenate(
        [jnp.where(tag == jnp.asarray(k, rows.dtype), rows, zero) for k in range(kinds_total)], axis=1
    )


def place_children_kernel(half, first, payload_ref, weight_ref, *rest):
    if first:
        out_ref, total_ref, rel_ref, code_ref, ends_vmem, ends_ref, sem = rest
    else:
        prior_ref, out_ref, total_ref, rel_ref, code_ref, ends_vmem, ends_ref, sem = rest
    par_rows, chan_out = out_ref.shape
    sources = payload_ref.shape[0]
    kinds_total = weight_ref.shape[0] // payload_ref.shape[2]
    lines = half // LANES
    size = min(2 * TILE, half)
    parts = size // TILE
    per = TILE // LANES
    window = min((5 if first else 3) * TILE // 2, par_rows)
    meta = payload_ref[:, half : half + ALIGN, :].astype(jnp.float32).astype(jnp.int32)
    rel = meta[:, 0:8] * 16 + (meta[:, 8:16] >> 3)
    line = lax.broadcasted_iota(jnp.int32, rel.shape, 1)
    rel = jnp.where(line < lines, rel, par_rows).reshape(8 * sources, LANES)
    rel_ref[...] = rel
    code_ref[...] = (meta[:, 8:16] & 7).reshape(8 * sources, LANES)
    least = jnp.min(jnp.maximum(rel, 0), axis=1, keepdims=True)
    most = jnp.max(jnp.where(rel < par_rows, rel, -1), axis=1, keepdims=True)
    for side, value in enumerate((least, most)):
        value = jnp.broadcast_to(value.astype(jnp.float32), rel.shape)
        if value.shape[0] % LANES:
            value = jnp.concatenate([value] * (LANES // value.shape[0]), axis=0)
        for i in range(value.shape[0] // LANES):
            turned = jnp.transpose(value[i * LANES : (i + 1) * LANES])
            ends_vmem[side, i] = turned[0:8].astype(jnp.int32)

    def end_of(side, line):
        return ends_ref[side, line // LANES, 0, line % LANES]

    copy = pltpu.make_async_copy(ends_vmem, ends_ref, sem)
    copy.start()
    total_ref[...] = jnp.zeros(total_ref.shape, jnp.float32)
    if not first:
        total_ref[:, 0:chan_out] = prior_ref[...]
    copy.wait()
    chunks = half // size

    def chunk(step, carry):
        s = step // chunks
        c = step % chunks
        line0 = 8 * s + c * (size // LANES)
        mosts = [
            jnp.maximum(end_of(1, line0 + per * p), end_of(1, line0 + per * p + per - 1))
            for p in range(parts)
        ]
        starts = [
            pl.multiple_of(jnp.minimum(end_of(0, line0 + per * p) // 8 * 8, par_rows - window), 8)
            for p in range(parts)
        ]
        slow = mosts[0] >= starts[0] + window
        live = mosts[0] >= 0
        for p in range(1, parts):
            slow = slow | (mosts[p] >= starts[p] + window)
            live = live | (mosts[p] >= 0)

        def work(extra):
            feats = payload_ref[s, pl.ds(pl.multiple_of(c * size, size), size), :]
            kinds = [column(code_ref[pl.ds(line0 + i, 1), :]) for i in range(size // LANES)]
            spread = spread_kinds(jnp.concatenate(kinds, axis=0), feats, kinds_total)
            product = jnp.dot(spread, weight_ref[...], preferred_element_type=jnp.float32)
            upper = product.astype(jnp.bfloat16)
            lower = (product - upper.astype(jnp.float32)).astype(jnp.bfloat16)
            both = jnp.concatenate([upper, lower], axis=1)
            for p in range(parts):
                count = TILE // LANES
                spots = [rel_ref[pl.ds(line0 + p * count + i, 1), :] for i in range(count)]
                spot = jnp.concatenate(spots, axis=1)
                mine = both[p * TILE : (p + 1) * TILE]

                def add(start, width, floor):
                    rank = lax.broadcasted_iota(jnp.int32, (width, TILE), 0) + start
                    hit = rank == spot
                    if floor is not None:
                        hit = hit & (rank >= floor)
                    total_ref[pl.ds(start, width), :] += jnp.dot(
                        jnp.where(hit, 1.0, 0.0).astype(jnp.bfloat16),
                        mine,
                        preferred_element_type=jnp.float32,
                    )

                add(starts[p], window, None)
                if extra:

                    def body(i, carry):
                        floor = starts[p] + window + i * TILE
                        add(pl.multiple_of(jnp.minimum(floor, par_rows - TILE), 8), TILE, floor)
                        return carry

                    lax.fori_loop(0, (mosts[p] + TILE - starts[p] - window) // TILE, body, 0)

        pl.when(live & slow)(lambda: work(True))
        pl.when(live & jnp.logical_not(slow))(lambda: work(False))
        return carry

    lax.fori_loop(0, sources * chunks, chunk, 0)
    out_ref[...] = (total_ref[:, 0:chan_out] + total_ref[:, chan_out : 2 * chan_out]).astype(out_ref.dtype)


def place_children(payload, weight_flat, prior, par_rows, last):
    first = prior is None
    chan_out = weight_flat.shape[1]
    sources = payload.shape[0]
    args = (payload, weight_flat) if first else (payload, weight_flat, prior)
    return pl.pallas_call(
        lambda *refs: place_children_kernel(payload.shape[1] - ALIGN, first, *refs),
        out_shape=jax.ShapeDtypeStruct((par_rows, chan_out), jnp.bfloat16 if last else jnp.float32),
        in_specs=[pl.BlockSpec(memory_space=pltpu.VMEM)] * len(args),
        out_specs=pl.BlockSpec(memory_space=pltpu.VMEM),
        scratch_shapes=[
            pltpu.VMEM((par_rows, 2 * chan_out), jnp.float32),
            pltpu.VMEM((8 * sources, LANES), jnp.int32),
            pltpu.VMEM((8 * sources, LANES), jnp.int32),
            pltpu.VMEM((2, -(-8 * sources // LANES), 8, LANES), jnp.int32),
            pltpu.SMEM((2, -(-8 * sources // LANES), 8, LANES), jnp.int32),
            pltpu.SemaphoreType.DMA(()),
        ],
        compiler_params=pltpu.CompilerParams(vmem_limit_bytes=VMEM_LIMIT),
        name="place_children",
    )(*args)


def stage_kernel(blocks, priors, shares, offset, table_ref, ends_ref, parent_ref, code_ref, feats_ref, weight_ref, *rest):
    cots = rest[:blocks]
    prior_refs = rest[blocks : blocks + priors]
    outs = rest[blocks + priors : 2 * blocks + priors]
    rest = rest[2 * blocks + priors :]
    terms_ref = rest[-1]
    kinds_total, chan_in, chan_out = terms_ref.shape
    size = 2 * TILE
    lines = size // LANES
    if priors:
        total = prior_refs[0][...]
        for prior_ref in prior_refs[1:]:
            total = total + prior_ref[...]
        terms_ref[...] = total
    else:
        terms_ref[...] = jnp.zeros(terms_ref.shape, jnp.float32)
    parents = parent_ref[...]
    for i, cot_ref in enumerate(cots):
        base = table_ref[offset + i]
        span = cot_ref.shape[0]
        window = min(3 * TILE, span)
        first = jnp.sum((parents < base).astype(jnp.int32)) // size
        last = (jnp.sum((parents < base + span).astype(jnp.int32)) + size - 1) // size

        def chunk(c, carry):
            starts, mosts = [], []
            for part in range(2):
                least = jnp.clip(ends_ref[0, 2 * c + part] - base, 0, span - 1)
                mosts.append(jnp.minimum(ends_ref[1, 2 * c + part] - base, span - 1))
                starts.append(pl.multiple_of(jnp.minimum(least // 16 * 16, span - window), 16))
            slow = (mosts[0] >= starts[0] + window) | (mosts[1] >= starts[1] + window)

            def work(extra):
                slots = (parent_ref[pl.ds(c * lines, lines), :] - base) * 8 + code_ref[
                    pl.ds(c * lines, lines), :
                ]
                slot = [column(slots[j : j + 1, :]) for j in range(lines)]
                kind = jnp.concatenate(slot, axis=0) & 7
                picked = []
                for part in range(2):
                    spot = jnp.concatenate(slot[2 * part : 2 * part + 2], axis=0) >> 3

                    def pull(start, width, floor):
                        lane = lax.broadcasted_iota(jnp.int32, (TILE, LANES), 1) + start
                        hits = []
                        for off in range(0, width, LANES):
                            hit = lane + off == spot
                            if floor is not None:
                                hit = hit & (lane + off >= floor)
                            hits.append(jnp.where(hit, 1.0, 0.0).astype(jnp.bfloat16))
                        return jnp.dot(
                            jnp.concatenate(hits, axis=1),
                            cot_ref[pl.ds(start, width), :],
                            preferred_element_type=jnp.float32,
                        )

                    rows = pull(starts[part], window, None)
                    if extra:

                        def body(n, rows):
                            floor = starts[part] + window + n * TILE
                            at = pl.multiple_of(jnp.minimum(floor, span - TILE), 16)
                            return rows + pull(at, TILE, floor)

                        count = (mosts[part] + TILE - starts[part] - window) // TILE
                        rows = lax.fori_loop(0, count, body, rows)
                    picked.append(rows.astype(jnp.bfloat16))
                spread = spread_kinds(kind, jnp.concatenate(picked, axis=0), kinds_total)
                there = pl.ds(pl.multiple_of((c - first) * size, size), size)
                outs[i][there, :] = jnp.dot(
                    spread, weight_ref[...], preferred_element_type=jnp.float32
                ).astype(jnp.bfloat16)
                part = lax.dot_general(
                    feats_ref[pl.ds(pl.multiple_of(c * size, size), size), :],
                    spread,
                    (((0,), (0,)), ((), ())),
                    preferred_element_type=jnp.float32,
                )
                for k in range(kinds_total):
                    terms_ref[k] += part[:, k * chan_out : (k + 1) * chan_out]

            pl.when(slow)(lambda: work(True))
            pl.when(jnp.logical_not(slow))(lambda: work(False))
            return carry

        lax.fori_loop(first, last, chunk, 0)
    if shares:
        per = kinds_total // shares
        for m in range(shares):
            owner = table_ref[offset + blocks + m]
            rest[m][...] = terms_ref[pl.ds(owner * per, per)].reshape(rest[m].shape)


def stage(table, offset, ends, parents, codes, feats, weight_tall, cots, priors, shares, rows):
    blocks = len(cots)
    chan_out = cots[0].shape[1]
    chan_in = feats.shape[1]
    kinds_total = weight_tall.shape[0] // chan_out
    smem = pl.BlockSpec(memory_space=pltpu.SMEM)
    vmem = pl.BlockSpec(memory_space=pltpu.VMEM)
    args = (table, ends, parents, codes, feats, weight_tall, *cots, *priors)
    outs = [jax.ShapeDtypeStruct((rows, chan_in), jnp.bfloat16)] * blocks
    scratch = []
    terms_shape = (kinds_total, chan_in, chan_out)
    if shares:
        outs += [jax.ShapeDtypeStruct((kinds_total * chan_in // shares, chan_out), jnp.float32)] * shares
        scratch = [pltpu.VMEM(terms_shape, jnp.float32)]
    else:
        outs += [jax.ShapeDtypeStruct(terms_shape, jnp.float32)]
    return pl.pallas_call(
        lambda *refs: stage_kernel(blocks, len(priors), shares, offset, *refs),
        out_shape=outs,
        in_specs=[smem, smem] + [vmem] * (len(args) - 2),
        out_specs=[vmem] * len(outs),
        scratch_shapes=scratch,
        compiler_params=pltpu.CompilerParams(vmem_limit_bytes=VMEM_LIMIT),
        name="fine_gradients",
    )(*args)


def merge_kernel(spans, offset, table_ref, parent_ref, *rest):
    out_ref = rest[-1]
    size = 2 * TILE
    out_ref[...] = jnp.zeros(out_ref.shape, out_ref.dtype)
    parents = parent_ref[...]
    for i, span in enumerate(spans):
        base = table_ref[offset + i]
        first = jnp.sum((parents < base).astype(jnp.int32)) // size
        last = (jnp.sum((parents < base + span).astype(jnp.int32)) + size - 1) // size

        def chunk(c, carry):
            here = pl.ds(pl.multiple_of(c * size, size), size)
            there = pl.ds(pl.multiple_of((c - first) * size, size), size)
            out_ref[here, :] = (
                out_ref[here, :].astype(jnp.float32) + rest[i][there, :].astype(jnp.float32)
            ).astype(out_ref.dtype)
            return carry

        lax.fori_loop(first, last, chunk, 0)


def merge(table, offset, parents, spans, parts, shape):
    vmem = pl.BlockSpec(memory_space=pltpu.VMEM)
    return pl.pallas_call(
        lambda *refs: merge_kernel(spans, offset, *refs),
        out_shape=jax.ShapeDtypeStruct(shape, jnp.bfloat16),
        in_specs=[pl.BlockSpec(memory_space=pltpu.SMEM)] + [vmem] * (1 + len(parts)),
        out_specs=vmem,
        compiler_params=pltpu.CompilerParams(vmem_limit_bytes=VMEM_LIMIT),
        name="merge_gradients",
    )(table, parents, *parts)

GATE_EARLY = 3
LAST = ("up", "dp", 1)


def after(value, *marks):
    return lax.optimization_barrier((value, *marks))[0]


def swap(value, mask, axis):
    size = lax.axis_size(axis)
    return lax.ppermute(value, axis, [(i, i ^ mask) for i in range(size)])


def pick(parts, index):
    return lax.dynamic_index_in_dim(parts, index, 0, keepdims=False)


def sum_terms(keep, send, mark):
    space_size = lax.axis_size("space")
    dp_size = lax.axis_size("dp")
    total = keep + swap(send, 1, "dp")
    trail = [("dp", 1)]
    steps = [("dp", 1 << b) for b in range(1, dp_size.bit_length() - 1)] + [("space", 1)]
    for axis, bit in steps:
        total = mark(("down", axis, bit), total)
        mine = lax.axis_index(axis) // bit % 2
        parts = total.reshape(2, total.shape[0] // 2, total.shape[1])
        total = pick(parts, mine) + swap(pick(parts, 1 - mine), bit, axis)
        trail.append((axis, bit))
    total = mark("across", total)
    if space_size == 8:
        total = (total + swap(total, 2, "space")) + (swap(total, 4, "space") + swap(total, 6, "space"))
    else:
        bit = 2
        while bit < space_size:
            total = total + swap(total, bit, "space")
            bit *= 2
    spot = lax.axis_index("dp") // 2 * 2 + lax.axis_index("space") % 2
    if dp_size == 4:
        total = mark("up", total)
        pairs = [(d * space_size + s, (d ^ 2) * space_size + (s ^ 1)) for d in range(4) for s in range(space_size)]
        by = [total, swap(total, 1, "space"), swap(total, 2, "dp"), lax.ppermute(total, ("dp", "space"), pairs)]
        wide = []
        for place in range(4):
            piece = by[0]
            for k in range(1, 4):
                piece = jnp.where(spot ^ k == place, by[k], piece)
            wide.append(piece)
        total = jnp.concatenate(wide, axis=0)
        trail = trail[:1]
    for axis, bit in trail[::-1]:
        total = mark(("up", axis, bit), total)
        mine = lax.axis_index(axis) // bit % 2
        other = swap(total, bit, axis)
        total = jnp.where(
            mine == 0, jnp.concatenate([total, other]), jnp.concatenate([other, total])
        )
    return total


def table_row(place, bit, cycle, par_rows):
    size = len(cycle)
    spot = cycle.index(place)
    row = [place * par_rows]
    for step in range(1, size // 2):
        row += [cycle[(spot - step) % size] * par_rows, cycle[(spot + step) % size] * par_rows]
    far = cycle[(spot + size // 2) % size] * par_rows
    return row + [far, far + par_rows // 2, bit, 1 - bit]


def per_device(features, child_parent, child_code, weight, out_grad):
    fine_rows = features[0]
    row_count = fine_rows.shape[0]
    parents = child_parent[0].reshape(row_count // LANES, LANES)
    codes = child_code[0].reshape(row_count // LANES, LANES)
    cotangent = out_grad[0]
    par_rows = cotangent.shape[0]
    kinds_total, chan_in, chan_out = weight.shape
    space_size = lax.axis_size("space")
    dp_size = lax.axis_size("dp")
    me = lax.axis_index("space")
    capacity = 2 * row_count // space_size
    weight_flat = weight.reshape(kinds_total * chan_in, chan_out)
    weight_tall = jnp.transpose(weight, (0, 2, 1)).reshape(kinds_total * chan_out, chan_in)
    steps = space_size // 2
    half = par_rows // 2
    cycle = list(range(0, space_size, 2)) + list(range(space_size - 1, 0, -2))
    ahead = [(cycle[i], cycle[(i + 1) % space_size]) for i in range(space_size)]
    behind = [(b, a) for a, b in ahead]
    dp_bit = lax.axis_index("dp") % 2
    table = jnp.asarray(
        [table_row(d, b, cycle, par_rows) for d in range(space_size) for b in range(2)], jnp.int32
    )
    table = lax.dynamic_index_in_dim(table, 2 * me + dp_bit, 0, keepdims=False)
    early, late = pack(parents, codes, fine_rows, space_size, capacity // 2, par_rows)

    tiles = child_parent[0].reshape(row_count // TILE, TILE)
    ends = jnp.stack([tiles[:, 0], tiles[:, TILE - 1]])
    size = 2 * TILE
    window_rows = (-(-(2 * row_count // space_size) // size) + 1) * size
    grads, spans, terms_parts = [], [], []

    def advance(step, blocks, shares=0):
        *parts, = stage(
            table, max(2 * step - 1, 0), ends, parents, codes, fine_rows, weight_tall, blocks,
            terms_parts if shares else (), shares, window_rows,
        )
        grads.extend(parts[: len(blocks)])
        spans.extend(block.shape[0] for block in blocks)
        return parts[len(blocks) :]

    def exchange(windows, mark):
        return lax.all_to_all(after(windows, mark), "space", 0, 0, tiled=True)

    right = left = cotangent
    blocks = (cotangent,)
    for step in range(1, steps + 1):
        if step == steps:
            right, left = right[:half], left[half:]
        right = lax.ppermute(right, "space", ahead)
        left = lax.ppermute(left, "space", behind)
        terms_parts += advance(step - 1, blocks)
        blocks = (right, left)
        if step < steps:
            right, left = lax.optimization_barrier((right, left, terms_parts[-1]))[:2]
        if step == GATE_EARLY:
            early = exchange(early, right)
    blocks = (blocks[0], after(blocks[1], terms_parts[-1]))
    keep, give = advance(steps, blocks, 2)
    late = lax.all_to_all(after(late, *blocks), "space", 0, 0, tiled=True)
    placed = place_children(after(early, keep), weight_flat, None, par_rows, False)
    acc = place_children(late, weight_flat, placed, par_rows, True)

    feature_grad = merge(table, 0, parents, spans, grads, fine_rows.shape)

    def mark(name, value):
        if name == ("down", "dp", 2):
            return after(value, placed)
        if name == LAST:
            return after(value, acc)
        return after(value, feature_grad) if name == "across" else value

    terms = sum_terms(keep, give, mark)
    total_rows = row_count * space_size * dp_size
    summed = terms.reshape(kinds_total, chan_in, chan_out)
    weight_grad = summed / jnp.sqrt(jnp.float32(total_rows))
    return (acc[None], feature_grad[None], weight_grad)


def solution(mesh):
    placed = (
        P("dp", "space", None),
        P("dp", "space"),
        P("dp", "space"),
        P(),
        P("dp", "space", None),
    )
    return jax.shard_map(
        per_device,
        mesh=mesh,
        in_specs=placed,
        out_specs=(P("dp", "space", None), P("dp", "space", None), P()),
        check_vma=False,
    )
```

```python
import jax
import jax.numpy as jnp
from jax import lax
from jax.experimental import pallas as pl
from jax.experimental.pallas import tpu as pltpu
from jax.sharding import PartitionSpec as P

LANES = 128
ALIGN = 16
TILE = 256
GROUP = 4
VMEM_LIMIT = 60 * 1024 * 1024


def column(row):
    return jnp.transpose(jnp.broadcast_to(row.astype(jnp.float32), (LANES, LANES))).astype(jnp.int32)


def pack_kernel(half, par_rows, parent_ref, code_ref, feats_ref, early_ref, late_ref, wide, parents, codes, stage_ref, sems):
    lines = parent_ref.shape[0]
    count = early_ref.shape[0]
    fine_rows = lines * LANES
    half_lines = half // LANES
    parents[...] = jnp.full(parents.shape, 1 << 20, jnp.int32)
    codes[...] = jnp.zeros(codes.shape, jnp.int32)
    parents[0:lines] = parent_ref[...]
    codes[0:lines] = code_ref[...]
    wide[0:fine_rows] = feats_ref[...].astype(jnp.float32)
    wide[fine_rows:] = jnp.zeros((wide.shape[0] - fine_rows, wide.shape[1]), jnp.float32)
    lane = lax.broadcasted_iota(jnp.int32, (8, LANES), 1)
    copies = []
    for m in range(count):
        base = m * par_rows
        start = jnp.sum((parent_ref[...] < base).astype(jnp.int32))
        for part, out in enumerate((early_ref, late_ref)):
            here = start + part * half
            line = here // LANES
            shift = here % LANES

            def window(ref):
                now = pltpu.roll(ref[pl.ds(line, 8), :], (LANES - shift) % LANES, 1)
                after = pltpu.roll(ref[pl.ds(line + 1, 8), :], (LANES - shift) % LANES, 1)
                return jnp.where(lane < LANES - shift, now, after)

            rel = window(parents) - base
            high = jnp.clip(rel >> 4, -1, 256)
            low = (rel & 15) * 8 + window(codes)
            both = jnp.concatenate([high, low], axis=0).astype(jnp.float32)
            stage_ref[m, part, 0:half] = wide[pl.ds(here, half), :].astype(jnp.bfloat16)
            stage_ref[m, part, half : half + ALIGN] = both.astype(jnp.bfloat16)
            copy = pltpu.make_async_copy(stage_ref.at[m, part], out.at[m], sems.at[m, part])
            copy.start()
            copies.append(copy)
    for copy in copies:
        copy.wait()


def pack(parents, codes, feats, count, half, par_rows):
    lines = parents.shape[0]
    rows = half + ALIGN
    vmem = pl.BlockSpec(memory_space=pltpu.VMEM)
    return pl.pallas_call(
        lambda *refs: pack_kernel(half, par_rows, *refs),
        out_shape=[jax.ShapeDtypeStruct((count, rows, LANES), jnp.bfloat16)] * 2,
        in_specs=[vmem] * 3,
        out_specs=[pl.BlockSpec(memory_space=pl.ANY)] * 2,
        scratch_shapes=[
            pltpu.VMEM((feats.shape[0] + 2 * half + 8, LANES), jnp.float32),
            pltpu.VMEM((lines + half // LANES + 16, LANES), jnp.int32),
            pltpu.VMEM((lines + half // LANES + 16, LANES), jnp.int32),
            pltpu.VMEM((count, 2, rows, LANES), jnp.bfloat16),
            pltpu.SemaphoreType.DMA((count, 2)),
        ],
        compiler_params=pltpu.CompilerParams(vmem_limit_bytes=VMEM_LIMIT),
        name="pack_windows",
    )(parents, codes, feats)


def spread_kinds(kind, rows, kinds_total):
    zero = jnp.zeros((), rows.dtype)
    tag = kind.astype(jnp.float32).astype(rows.dtype)
    return jnp.concatenate(
        [jnp.where(tag == jnp.asarray(k, rows.dtype), rows, zero) for k in range(kinds_total)], axis=1
    )


def place_children_kernel(half, first, payload_ref, weight_ref, *rest):
    if first:
        out_ref, total_ref, rel_ref, code_ref, ends_vmem, ends_ref, list_ref, sem = rest
    else:
        prior_ref, out_ref, total_ref, rel_ref, code_ref, ends_vmem, ends_ref, list_ref, sem = rest
    par_rows, chan_out = out_ref.shape
    sources = payload_ref.shape[0]
    kinds_total = weight_ref.shape[0] // payload_ref.shape[2]
    lines = half // LANES
    per = TILE // LANES
    window = min((5 if first else 3) * TILE // 2, par_rows)
    meta = payload_ref[:, half : half + ALIGN, :].astype(jnp.float32).astype(jnp.int32)
    rel = meta[:, 0:8] * 16 + (meta[:, 8:16] >> 3)
    line = lax.broadcasted_iota(jnp.int32, rel.shape, 1)
    rel = jnp.where(line < lines, rel, par_rows).reshape(8 * sources, LANES)
    rel_ref[...] = rel
    code_ref[...] = (meta[:, 8:16] & 7).reshape(8 * sources, LANES)
    least = jnp.min(jnp.maximum(rel, 0), axis=1, keepdims=True)
    most = jnp.max(jnp.where(rel < par_rows, rel, -1), axis=1, keepdims=True)
    for side, value in enumerate((least, most)):
        value = jnp.broadcast_to(value.astype(jnp.float32), rel.shape)
        if value.shape[0] % LANES:
            value = jnp.concatenate([value] * (LANES // value.shape[0]), axis=0)
        for i in range(value.shape[0] // LANES):
            turned = jnp.transpose(value[i * LANES : (i + 1) * LANES])
            ends_vmem[side, i] = turned[0:8].astype(jnp.int32)

    def end_of(side, line):
        return ends_ref[side, line // LANES, 0, line % LANES]

    copy = pltpu.make_async_copy(ends_vmem, ends_ref, sem)
    copy.start()
    total_ref[...] = jnp.zeros(total_ref.shape, jnp.float32)
    if not first:
        total_ref[:, 0:chan_out] = prior_ref[...]
    copy.wait()
    tiles = half // TILE

    def collect(tile, found):
        line = 8 * (tile // tiles) + per * (tile % tiles)
        live = jnp.maximum(end_of(1, line), end_of(1, line + per - 1)) >= 0

        @pl.when(live)
        def _():
            list_ref[found] = line

        return found + live.astype(jnp.int32)

    found = lax.fori_loop(0, sources * tiles, collect, 0)

    def group(step, carry):
        held, mosts, starts, spare = [], [], [], []
        slow = False
        for p in range(GROUP):
            index = step * GROUP + p
            line = list_ref[jnp.minimum(index, found - 1)]
            most = jnp.maximum(end_of(1, line), end_of(1, line + per - 1))
            start = pl.multiple_of(jnp.minimum(end_of(0, line) // 8 * 8, par_rows - window), 8)
            held.append(line)
            starts.append(start)
            mosts.append(jnp.where(index < found, most, -1))
            spare.append(jnp.where(index < found, 0, 1 << 20))
            slow = slow | (mosts[p] >= start + window)

        def work(extra):
            feats, kinds = [], []
            for line in held:
                row0 = pl.multiple_of(line % 8 * LANES, TILE)
                feats.append(payload_ref[line // 8, pl.ds(row0, TILE), :])
                kinds += [column(code_ref[pl.ds(line + i, 1), :]) for i in range(per)]
            spread = spread_kinds(
                jnp.concatenate(kinds, axis=0), jnp.concatenate(feats, axis=0), kinds_total
            )
            product = jnp.dot(spread, weight_ref[...], preferred_element_type=jnp.float32)
            upper = product.astype(jnp.bfloat16)
            lower = (product - upper.astype(jnp.float32)).astype(jnp.bfloat16)
            both = jnp.concatenate([upper, lower], axis=1)
            for p in range(GROUP):
                spots = [rel_ref[pl.ds(held[p] + i, 1), :] for i in range(per)]
                spot = jnp.concatenate(spots, axis=1) + spare[p]
                mine = both[p * TILE : (p + 1) * TILE]

                def add(start, width, floor):
                    rank = lax.broadcasted_iota(jnp.int32, (width, TILE), 0) + start
                    hit = rank == spot
                    if floor is not None:
                        hit = hit & (rank >= floor)
                    total_ref[pl.ds(start, width), :] += jnp.dot(
                        jnp.where(hit, 1.0, 0.0).astype(jnp.bfloat16),
                        mine,
                        preferred_element_type=jnp.float32,
                    )

                add(starts[p], window, None)
                if extra:

                    def body(i, carry):
                        floor = starts[p] + window + i * TILE
                        add(pl.multiple_of(jnp.minimum(floor, par_rows - TILE), 8), TILE, floor)
                        return carry

                    lax.fori_loop(0, (mosts[p] + TILE - starts[p] - window) // TILE, body, 0)

        pl.when(slow)(lambda: work(True))
        pl.when(jnp.logical_not(slow))(lambda: work(False))
        return carry

    lax.fori_loop(0, (found + GROUP - 1) // GROUP, group, 0)
    out_ref[...] = (total_ref[:, 0:chan_out] + total_ref[:, chan_out : 2 * chan_out]).astype(out_ref.dtype)


def place_children(payload, weight_flat, prior, par_rows, last):
    first = prior is None
    chan_out = weight_flat.shape[1]
    sources = payload.shape[0]
    args = (payload, weight_flat) if first else (payload, weight_flat, prior)
    return pl.pallas_call(
        lambda *refs: place_children_kernel(payload.shape[1] - ALIGN, first, *refs),
        out_shape=jax.ShapeDtypeStruct((par_rows, chan_out), jnp.bfloat16 if last else jnp.float32),
        in_specs=[pl.BlockSpec(memory_space=pltpu.VMEM)] * len(args),
        out_specs=pl.BlockSpec(memory_space=pltpu.VMEM),
        scratch_shapes=[
            pltpu.VMEM((par_rows, 2 * chan_out), jnp.float32),
            pltpu.VMEM((8 * sources, LANES), jnp.int32),
            pltpu.VMEM((8 * sources, LANES), jnp.int32),
            pltpu.VMEM((2, -(-8 * sources // LANES), 8, LANES), jnp.int32),
            pltpu.SMEM((2, -(-8 * sources // LANES), 8, LANES), jnp.int32),
            pltpu.SMEM((4 * sources,), jnp.int32),
            pltpu.SemaphoreType.DMA(()),
        ],
        compiler_params=pltpu.CompilerParams(vmem_limit_bytes=VMEM_LIMIT),
        name="place_children",
    )(*args)


def stage_kernel(blocks, priors, shares, offset, table_ref, ends_ref, parent_ref, code_ref, feats_ref, weight_ref, *rest):
    cots = rest[:blocks]
    prior_refs = rest[blocks : blocks + priors]
    outs = rest[blocks + priors : 2 * blocks + priors]
    rest = rest[2 * blocks + priors :]
    terms_ref = rest[-1]
    kinds_total, chan_in, chan_out = terms_ref.shape
    size = 2 * TILE
    lines = size // LANES
    if priors:
        total = prior_refs[0][...]
        for prior_ref in prior_refs[1:]:
            total = total + prior_ref[...]
        terms_ref[...] = total
    else:
        terms_ref[...] = jnp.zeros(terms_ref.shape, jnp.float32)
    parents = parent_ref[...]
    for i, cot_ref in enumerate(cots):
        base = table_ref[offset + i]
        span = cot_ref.shape[0]
        window = min(3 * TILE, span)
        first = jnp.sum((parents < base).astype(jnp.int32)) // size
        last = (jnp.sum((parents < base + span).astype(jnp.int32)) + size - 1) // size

        def chunk(c, carry):
            starts, mosts = [], []
            for part in range(2):
                least = jnp.clip(ends_ref[0, 2 * c + part] - base, 0, span - 1)
                mosts.append(jnp.minimum(ends_ref[1, 2 * c + part] - base, span - 1))
                starts.append(pl.multiple_of(jnp.minimum(least // 16 * 16, span - window), 16))
            slow = (mosts[0] >= starts[0] + window) | (mosts[1] >= starts[1] + window)

            def work(extra):
                slots = (parent_ref[pl.ds(c * lines, lines), :] - base) * 8 + code_ref[
                    pl.ds(c * lines, lines), :
                ]
                slot = [column(slots[j : j + 1, :]) for j in range(lines)]
                kind = jnp.concatenate(slot, axis=0) & 7
                picked = []
                for part in range(2):
                    spot = jnp.concatenate(slot[2 * part : 2 * part + 2], axis=0) >> 3

                    def pull(start, width, floor):
                        lane = lax.broadcasted_iota(jnp.int32, (TILE, LANES), 1) + start
                        hits = []
                        for off in range(0, width, LANES):
                            hit = lane + off == spot
                            if floor is not None:
                                hit = hit & (lane + off >= floor)
                            hits.append(jnp.where(hit, 1.0, 0.0).astype(jnp.bfloat16))
                        return jnp.dot(
                            jnp.concatenate(hits, axis=1),
                            cot_ref[pl.ds(start, width), :],
                            preferred_element_type=jnp.float32,
                        )

                    rows = pull(starts[part], window, None)
                    if extra:

                        def body(n, rows):
                            floor = starts[part] + window + n * TILE
                            at = pl.multiple_of(jnp.minimum(floor, span - TILE), 16)
                            return rows + pull(at, TILE, floor)

                        count = (mosts[part] + TILE - starts[part] - window) // TILE
                        rows = lax.fori_loop(0, count, body, rows)
                    picked.append(rows.astype(jnp.bfloat16))
                spread = spread_kinds(kind, jnp.concatenate(picked, axis=0), kinds_total)
                there = pl.ds(pl.multiple_of((c - first) * size, size), size)
                outs[i][there, :] = jnp.dot(
                    spread, weight_ref[...], preferred_element_type=jnp.float32
                ).astype(jnp.bfloat16)
                part = lax.dot_general(
                    feats_ref[pl.ds(pl.multiple_of(c * size, size), size), :],
                    spread,
                    (((0,), (0,)), ((), ())),
                    preferred_element_type=jnp.float32,
                )
                for k in range(kinds_total):
                    terms_ref[k] += part[:, k * chan_out : (k + 1) * chan_out]

            pl.when(slow)(lambda: work(True))
            pl.when(jnp.logical_not(slow))(lambda: work(False))
            return carry

        lax.fori_loop(first, last, chunk, 0)
    if shares:
        per = kinds_total // shares
        for m in range(shares):
            owner = table_ref[offset + blocks + m]
            rest[m][...] = terms_ref[pl.ds(owner * per, per)].reshape(rest[m].shape)


def stage(table, offset, ends, parents, codes, feats, weight_tall, cots, priors, shares, rows):
    blocks = len(cots)
    chan_out = cots[0].shape[1]
    chan_in = feats.shape[1]
    kinds_total = weight_tall.shape[0] // chan_out
    smem = pl.BlockSpec(memory_space=pltpu.SMEM)
    vmem = pl.BlockSpec(memory_space=pltpu.VMEM)
    args = (table, ends, parents, codes, feats, weight_tall, *cots, *priors)
    outs = [jax.ShapeDtypeStruct((rows, chan_in), jnp.bfloat16)] * blocks
    scratch = []
    terms_shape = (kinds_total, chan_in, chan_out)
    if shares:
        outs += [jax.ShapeDtypeStruct((kinds_total * chan_in // shares, chan_out), jnp.float32)] * shares
        scratch = [pltpu.VMEM(terms_shape, jnp.float32)]
    else:
        outs += [jax.ShapeDtypeStruct(terms_shape, jnp.float32)]
    return pl.pallas_call(
        lambda *refs: stage_kernel(blocks, len(priors), shares, offset, *refs),
        out_shape=outs,
        in_specs=[smem, smem] + [vmem] * (len(args) - 2),
        out_specs=[vmem] * len(outs),
        scratch_shapes=scratch,
        compiler_params=pltpu.CompilerParams(vmem_limit_bytes=VMEM_LIMIT),
        name="fine_gradients",
    )(*args)


def merge_kernel(spans, offset, table_ref, parent_ref, *rest):
    out_ref = rest[-1]
    size = 2 * TILE
    out_ref[...] = jnp.zeros(out_ref.shape, out_ref.dtype)
    parents = parent_ref[...]
    for i, span in enumerate(spans):
        base = table_ref[offset + i]
        first = jnp.sum((parents < base).astype(jnp.int32)) // size
        last = (jnp.sum((parents < base + span).astype(jnp.int32)) + size - 1) // size

        def chunk(c, carry):
            here = pl.ds(pl.multiple_of(c * size, size), size)
            there = pl.ds(pl.multiple_of((c - first) * size, size), size)
            out_ref[here, :] = (
                out_ref[here, :].astype(jnp.float32) + rest[i][there, :].astype(jnp.float32)
            ).astype(out_ref.dtype)
            return carry

        lax.fori_loop(first, last, chunk, 0)


def merge(table, offset, parents, spans, parts, shape):
    vmem = pl.BlockSpec(memory_space=pltpu.VMEM)
    return pl.pallas_call(
        lambda *refs: merge_kernel(spans, offset, *refs),
        out_shape=jax.ShapeDtypeStruct(shape, jnp.bfloat16),
        in_specs=[pl.BlockSpec(memory_space=pltpu.SMEM)] + [vmem] * (1 + len(parts)),
        out_specs=vmem,
        compiler_params=pltpu.CompilerParams(vmem_limit_bytes=VMEM_LIMIT),
        name="merge_gradients",
    )(table, parents, *parts)

GATE_EARLY = 3
LAST = ("up", "dp", 1)


def after(value, *marks):
    return lax.optimization_barrier((value, *marks))[0]


def swap(value, mask, axis):
    size = lax.axis_size(axis)
    return lax.ppermute(value, axis, [(i, i ^ mask) for i in range(size)])


def pick(parts, index):
    return lax.dynamic_index_in_dim(parts, index, 0, keepdims=False)


def sum_terms(keep, send, mark):
    space_size = lax.axis_size("space")
    dp_size = lax.axis_size("dp")
    total = keep + swap(send, 1, "dp")
    trail = [("dp", 1)]
    steps = [("dp", 1 << b) for b in range(1, dp_size.bit_length() - 1)] + [("space", 1)]
    for axis, bit in steps:
        total = mark(("down", axis, bit), total)
        mine = lax.axis_index(axis) // bit % 2
        parts = total.reshape(2, total.shape[0] // 2, total.shape[1])
        total = pick(parts, mine) + swap(pick(parts, 1 - mine), bit, axis)
        trail.append((axis, bit))
    total = mark("across", total)
    if space_size == 8:
        total = (total + swap(total, 2, "space")) + (swap(total, 4, "space") + swap(total, 6, "space"))
    else:
        bit = 2
        while bit < space_size:
            total = total + swap(total, bit, "space")
            bit *= 2
    spot = lax.axis_index("dp") // 2 * 2 + lax.axis_index("space") % 2
    if dp_size == 4:
        total = mark("up", total)
        pairs = [(d * space_size + s, (d ^ 2) * space_size + (s ^ 1)) for d in range(4) for s in range(space_size)]
        by = [total, swap(total, 1, "space"), swap(total, 2, "dp"), lax.ppermute(total, ("dp", "space"), pairs)]
        wide = []
        for place in range(4):
            piece = by[0]
            for k in range(1, 4):
                piece = jnp.where(spot ^ k == place, by[k], piece)
            wide.append(piece)
        total = jnp.concatenate(wide, axis=0)
        trail = trail[:1]
    for axis, bit in trail[::-1]:
        total = mark(("up", axis, bit), total)
        mine = lax.axis_index(axis) // bit % 2
        other = swap(total, bit, axis)
        total = jnp.where(
            mine == 0, jnp.concatenate([total, other]), jnp.concatenate([other, total])
        )
    return total


def table_row(place, bit, cycle, par_rows):
    size = len(cycle)
    spot = cycle.index(place)
    row = [place * par_rows]
    for step in range(1, size // 2):
        row += [cycle[(spot - step) % size] * par_rows, cycle[(spot + step) % size] * par_rows]
    far = cycle[(spot + size // 2) % size] * par_rows
    return row + [far, far + par_rows // 2, bit, 1 - bit]


def per_device(features, child_parent, child_code, weight, out_grad):
    fine_rows = features[0]
    row_count = fine_rows.shape[0]
    parents = child_parent[0].reshape(row_count // LANES, LANES)
    codes = child_code[0].reshape(row_count // LANES, LANES)
    cotangent = out_grad[0]
    par_rows = cotangent.shape[0]
    kinds_total, chan_in, chan_out = weight.shape
    space_size = lax.axis_size("space")
    dp_size = lax.axis_size("dp")
    me = lax.axis_index("space")
    capacity = 2 * row_count // space_size
    weight_flat = weight.reshape(kinds_total * chan_in, chan_out)
    weight_tall = jnp.transpose(weight, (0, 2, 1)).reshape(kinds_total * chan_out, chan_in)
    steps = space_size // 2
    half = par_rows // 2
    cycle = list(range(0, space_size, 2)) + list(range(space_size - 1, 0, -2))
    ahead = [(cycle[i], cycle[(i + 1) % space_size]) for i in range(space_size)]
    behind = [(b, a) for a, b in ahead]
    dp_bit = lax.axis_index("dp") % 2
    table = jnp.asarray(
        [table_row(d, b, cycle, par_rows) for d in range(space_size) for b in range(2)], jnp.int32
    )
    table = lax.dynamic_index_in_dim(table, 2 * me + dp_bit, 0, keepdims=False)
    early, late = pack(parents, codes, fine_rows, space_size, capacity // 2, par_rows)

    tiles = child_parent[0].reshape(row_count // TILE, TILE)
    ends = jnp.stack([tiles[:, 0], tiles[:, TILE - 1]])
    size = 2 * TILE
    window_rows = (-(-(2 * row_count // space_size) // size) + 1) * size
    grads, spans, terms_parts = [], [], []

    def advance(step, blocks, shares=0):
        *parts, = stage(
            table, max(2 * step - 1, 0), ends, parents, codes, fine_rows, weight_tall, blocks,
            terms_parts if shares else (), shares, window_rows,
        )
        grads.extend(parts[: len(blocks)])
        spans.extend(block.shape[0] for block in blocks)
        return parts[len(blocks) :]

    def exchange(windows, mark):
        return lax.all_to_all(after(windows, mark), "space", 0, 0, tiled=True)

    right = left = cotangent
    blocks = (cotangent,)
    for step in range(1, steps + 1):
        if step == steps:
            right, left = right[:half], left[half:]
        right = lax.ppermute(right, "space", ahead)
        left = lax.ppermute(left, "space", behind)
        terms_parts += advance(step - 1, blocks)
        blocks = (right, left)
        if step < steps:
            right, left = lax.optimization_barrier((right, left, terms_parts[-1]))[:2]
        if step == GATE_EARLY:
            early = exchange(early, right)
    blocks = (blocks[0], after(blocks[1], terms_parts[-1]))
    keep, give = advance(steps, blocks, 2)
    late = lax.all_to_all(after(late, *blocks), "space", 0, 0, tiled=True)
    placed = place_children(after(early, keep), weight_flat, None, par_rows, False)
    acc = place_children(late, weight_flat, placed, par_rows, True)

    feature_grad = merge(table, 0, parents, spans, grads, fine_rows.shape)

    def mark(name, value):
        if name == ("down", "dp", 2):
            return after(value, placed)
        if name == LAST:
            return after(value, acc)
        return after(value, feature_grad) if name == "across" else value

    terms = sum_terms(keep, give, mark)
    total_rows = row_count * space_size * dp_size
    summed = terms.reshape(kinds_total, chan_in, chan_out)
    weight_grad = summed / jnp.sqrt(jnp.float32(total_rows))
    return (acc[None], feature_grad[None], weight_grad)


def solution(mesh):
    placed = (
        P("dp", "space", None),
        P("dp", "space"),
        P("dp", "space"),
        P(),
        P("dp", "space", None),
    )
    return jax.shard_map(
        per_device,
        mesh=mesh,
        in_specs=placed,
        out_specs=(P("dp", "space", None), P("dp", "space", None), P()),
        check_vma=False,
    )
```

```python
import jax
import jax.numpy as jnp
from jax import lax
from jax.experimental import pallas as pl
from jax.experimental.pallas import tpu as pltpu
from jax.sharding import PartitionSpec as P

LANES = 128
ALIGN = 16
TILE = 256
VMEM_LIMIT = 60 * 1024 * 1024


def column(row):
    return jnp.transpose(jnp.broadcast_to(row.astype(jnp.float32), (LANES, LANES))).astype(jnp.int32)


def pack_kernel(half, par_rows, parent_ref, code_ref, feats_ref, early_ref, late_ref, wide, parents, codes, stage_ref, sems):
    lines = parent_ref.shape[0]
    count = early_ref.shape[0]
    fine_rows = lines * LANES
    half_lines = half // LANES
    parents[...] = jnp.full(parents.shape, 1 << 20, jnp.int32)
    codes[...] = jnp.zeros(codes.shape, jnp.int32)
    parents[0:lines] = parent_ref[...]
    codes[0:lines] = code_ref[...]
    wide[0:fine_rows] = feats_ref[...].astype(jnp.float32)
    wide[fine_rows:] = jnp.zeros((wide.shape[0] - fine_rows, wide.shape[1]), jnp.float32)
    lane = lax.broadcasted_iota(jnp.int32, (8, LANES), 1)
    copies = []
    for m in range(count):
        base = m * par_rows
        start = jnp.sum((parent_ref[...] < base).astype(jnp.int32))
        for part, out in enumerate((early_ref, late_ref)):
            here = start + part * half
            line = here // LANES
            shift = here % LANES

            def window(ref):
                now = pltpu.roll(ref[pl.ds(line, 8), :], (LANES - shift) % LANES, 1)
                after = pltpu.roll(ref[pl.ds(line + 1, 8), :], (LANES - shift) % LANES, 1)
                return jnp.where(lane < LANES - shift, now, after)

            rel = window(parents) - base
            high = jnp.clip(rel >> 4, -1, 256)
            low = (rel & 15) * 8 + window(codes)
            both = jnp.concatenate([high, low], axis=0).astype(jnp.float32)
            stage_ref[m, part, 0:half] = wide[pl.ds(here, half), :].astype(jnp.bfloat16)
            stage_ref[m, part, half : half + ALIGN] = both.astype(jnp.bfloat16)
            copy = pltpu.make_async_copy(stage_ref.at[m, part], out.at[m], sems.at[m, part])
            copy.start()
            copies.append(copy)
    for copy in copies:
        copy.wait()


def pack(parents, codes, feats, count, half, par_rows):
    lines = parents.shape[0]
    rows = half + ALIGN
    vmem = pl.BlockSpec(memory_space=pltpu.VMEM)
    return pl.pallas_call(
        lambda *refs: pack_kernel(half, par_rows, *refs),
        out_shape=[jax.ShapeDtypeStruct((count, rows, LANES), jnp.bfloat16)] * 2,
        in_specs=[vmem] * 3,
        out_specs=[pl.BlockSpec(memory_space=pl.ANY)] * 2,
        scratch_shapes=[
            pltpu.VMEM((feats.shape[0] + 2 * half + 8, LANES), jnp.float32),
            pltpu.VMEM((lines + half // LANES + 16, LANES), jnp.int32),
            pltpu.VMEM((lines + half // LANES + 16, LANES), jnp.int32),
            pltpu.VMEM((count, 2, rows, LANES), jnp.bfloat16),
            pltpu.SemaphoreType.DMA((count, 2)),
        ],
        compiler_params=pltpu.CompilerParams(vmem_limit_bytes=VMEM_LIMIT),
        name="pack_windows",
    )(parents, codes, feats)


def spread_kinds(kind, rows, kinds_total):
    zero = jnp.zeros((), rows.dtype)
    tag = kind.astype(jnp.float32).astype(rows.dtype)
    return jnp.concatenate(
        [jnp.where(tag == jnp.asarray(k, rows.dtype), rows, zero) for k in range(kinds_total)], axis=1
    )


def place_children_kernel(half, first, payload_ref, weight_ref, *rest):
    if first:
        out_ref, total_ref, rel_ref, code_ref, ends_vmem, ends_ref, list_ref, sem = rest
    else:
        prior_ref, out_ref, total_ref, rel_ref, code_ref, ends_vmem, ends_ref, list_ref, sem = rest
    par_rows, chan_out = out_ref.shape
    sources = payload_ref.shape[0]
    kinds_total = weight_ref.shape[0] // payload_ref.shape[2]
    lines = half // LANES
    per = TILE // LANES
    window = min((5 if first else 3) * TILE // 2, par_rows)
    meta = payload_ref[:, half : half + ALIGN, :].astype(jnp.float32).astype(jnp.int32)
    rel = meta[:, 0:8] * 16 + (meta[:, 8:16] >> 3)
    line = lax.broadcasted_iota(jnp.int32, rel.shape, 1)
    rel = jnp.where(line < lines, rel, par_rows).reshape(8 * sources, LANES)
    rel_ref[...] = rel
    code_ref[...] = (meta[:, 8:16] & 7).reshape(8 * sources, LANES)
    least = jnp.min(jnp.maximum(rel, 0), axis=1, keepdims=True)
    most = jnp.max(jnp.where(rel < par_rows, rel, -1), axis=1, keepdims=True)
    for side, value in enumerate((least, most)):
        value = jnp.broadcast_to(value.astype(jnp.float32), rel.shape)
        if value.shape[0] % LANES:
            value = jnp.concatenate([value] * (LANES // value.shape[0]), axis=0)
        for i in range(value.shape[0] // LANES):
            turned = jnp.transpose(value[i * LANES : (i + 1) * LANES])
            ends_vmem[side, i] = turned[0:8].astype(jnp.int32)

    def end_of(side, line):
        return ends_ref[side, line // LANES, 0, line % LANES]

    copy = pltpu.make_async_copy(ends_vmem, ends_ref, sem)
    copy.start()
    blank = jnp.zeros((par_rows, chan_out), jnp.float32)
    total_ref[:, 0:chan_out] = blank if first else prior_ref[...]
    total_ref[:, chan_out : 2 * chan_out] = blank
    copy.wait()
    tiles = half // TILE
    together = 4 if first else 6

    def collect(tile, found):
        line = 8 * (tile // tiles) + per * (tile % tiles)
        live = jnp.maximum(end_of(1, line), end_of(1, line + per - 1)) >= 0

        @pl.when(live)
        def _():
            list_ref[found] = line

        return found + live.astype(jnp.int32)

    found = lax.fori_loop(0, sources * tiles, collect, 0)

    def group(step, carry):
        held, mosts, starts, spare = [], [], [], []
        slow = False
        for p in range(together):
            index = step * together + p
            line = list_ref[jnp.minimum(index, found - 1)]
            most = jnp.maximum(end_of(1, line), end_of(1, line + per - 1))
            start = pl.multiple_of(jnp.minimum(end_of(0, line) // 8 * 8, par_rows - window), 8)
            held.append(line)
            starts.append(start)
            mosts.append(jnp.where(index < found, most, -1))
            spare.append(jnp.where(index < found, 0, 1 << 20))
            slow = slow | (mosts[p] >= start + window)

        def work(extra):
            feats, kinds = [], []
            for line in held:
                row0 = pl.multiple_of(line % 8 * LANES, TILE)
                feats.append(payload_ref[line // 8, pl.ds(row0, TILE), :])
                kinds += [column(code_ref[pl.ds(line + i, 1), :]) for i in range(per)]
            spread = spread_kinds(
                jnp.concatenate(kinds, axis=0), jnp.concatenate(feats, axis=0), kinds_total
            )
            product = jnp.dot(spread, weight_ref[...], preferred_element_type=jnp.float32)
            upper = product.astype(jnp.bfloat16)
            lower = (product - upper.astype(jnp.float32)).astype(jnp.bfloat16)
            both = jnp.concatenate([upper, lower], axis=1)
            for p in range(together):
                spots = [rel_ref[pl.ds(held[p] + i, 1), :] for i in range(per)]
                spot = jnp.concatenate(spots, axis=1) + spare[p]
                mine = both[p * TILE : (p + 1) * TILE]

                def add(start, width, floor):
                    rank = lax.broadcasted_iota(jnp.int32, (width, TILE), 0) + start
                    hit = rank == spot
                    if floor is not None:
                        hit = hit & (rank >= floor)
                    total_ref[pl.ds(start, width), :] += jnp.dot(
                        jnp.where(hit, 1.0, 0.0).astype(jnp.bfloat16),
                        mine,
                        preferred_element_type=jnp.float32,
                    )

                add(starts[p], window, None)
                if extra:

                    def body(i, carry):
                        floor = starts[p] + window + i * TILE
                        add(pl.multiple_of(jnp.minimum(floor, par_rows - TILE), 8), TILE, floor)
                        return carry

                    lax.fori_loop(0, (mosts[p] + TILE - starts[p] - window) // TILE, body, 0)

        pl.when(slow)(lambda: work(True))
        pl.when(jnp.logical_not(slow))(lambda: work(False))
        return carry

    lax.fori_loop(0, (found + together - 1) // together, group, 0)
    out_ref[...] = (total_ref[:, 0:chan_out] + total_ref[:, chan_out : 2 * chan_out]).astype(out_ref.dtype)


def place_children(payload, weight_flat, prior, par_rows, last):
    first = prior is None
    chan_out = weight_flat.shape[1]
    sources = payload.shape[0]
    args = (payload, weight_flat) if first else (payload, weight_flat, prior)
    return pl.pallas_call(
        lambda *refs: place_children_kernel(payload.shape[1] - ALIGN, first, *refs),
        out_shape=jax.ShapeDtypeStruct((par_rows, chan_out), jnp.bfloat16 if last else jnp.float32),
        in_specs=[pl.BlockSpec(memory_space=pltpu.VMEM)] * len(args),
        out_specs=pl.BlockSpec(memory_space=pltpu.VMEM),
        scratch_shapes=[
            pltpu.VMEM((par_rows, 2 * chan_out), jnp.float32),
            pltpu.VMEM((8 * sources, LANES), jnp.int32),
            pltpu.VMEM((8 * sources, LANES), jnp.int32),
            pltpu.VMEM((2, -(-8 * sources // LANES), 8, LANES), jnp.int32),
            pltpu.SMEM((2, -(-8 * sources // LANES), 8, LANES), jnp.int32),
            pltpu.SMEM((4 * sources,), jnp.int32),
            pltpu.SemaphoreType.DMA(()),
        ],
        compiler_params=pltpu.CompilerParams(vmem_limit_bytes=VMEM_LIMIT),
        name="place_children",
    )(*args)


def stage_kernel(blocks, priors, shares, offset, table_ref, ends_ref, parent_ref, code_ref, feats_ref, weight_ref, *rest):
    cots = rest[:blocks]
    prior_refs = rest[blocks : blocks + priors]
    outs = rest[blocks + priors : 2 * blocks + priors]
    rest = rest[2 * blocks + priors :]
    terms_ref = rest[-1]
    kinds_total, chan_in, chan_out = terms_ref.shape
    size = 2 * TILE
    lines = size // LANES
    if priors:
        total = prior_refs[0][...]
        for prior_ref in prior_refs[1:]:
            total = total + prior_ref[...]
        terms_ref[...] = total
    else:
        terms_ref[...] = jnp.zeros(terms_ref.shape, jnp.float32)
    parents = parent_ref[...]
    for i, cot_ref in enumerate(cots):
        base = table_ref[offset + i]
        span = cot_ref.shape[0]
        window = min(3 * TILE, span)
        first = jnp.sum((parents < base).astype(jnp.int32)) // size
        last = (jnp.sum((parents < base + span).astype(jnp.int32)) + size - 1) // size

        def chunk(c, carry):
            starts, mosts = [], []
            for part in range(2):
                least = jnp.clip(ends_ref[0, 2 * c + part] - base, 0, span - 1)
                mosts.append(jnp.minimum(ends_ref[1, 2 * c + part] - base, span - 1))
                starts.append(pl.multiple_of(jnp.minimum(least // 16 * 16, span - window), 16))
            slow = (mosts[0] >= starts[0] + window) | (mosts[1] >= starts[1] + window)

            def work(extra):
                slots = (parent_ref[pl.ds(c * lines, lines), :] - base) * 8 + code_ref[
                    pl.ds(c * lines, lines), :
                ]
                slot = [column(slots[j : j + 1, :]) for j in range(lines)]
                kind = jnp.concatenate(slot, axis=0) & 7
                picked = []
                for part in range(2):
                    spot = jnp.concatenate(slot[2 * part : 2 * part + 2], axis=0) >> 3

                    def pull(start, width, floor):
                        lane = lax.broadcasted_iota(jnp.int32, (TILE, LANES), 1) + start
                        hits = []
                        for off in range(0, width, LANES):
                            hit = lane + off == spot
                            if floor is not None:
                                hit = hit & (lane + off >= floor)
                            hits.append(jnp.where(hit, 1.0, 0.0).astype(jnp.bfloat16))
                        return jnp.dot(
                            jnp.concatenate(hits, axis=1),
                            cot_ref[pl.ds(start, width), :],
                            preferred_element_type=jnp.float32,
                        )

                    rows = pull(starts[part], window, None)
                    if extra:

                        def body(n, rows):
                            floor = starts[part] + window + n * TILE
                            at = pl.multiple_of(jnp.minimum(floor, span - TILE), 16)
                            return rows + pull(at, TILE, floor)

                        count = (mosts[part] + TILE - starts[part] - window) // TILE
                        rows = lax.fori_loop(0, count, body, rows)
                    picked.append(rows.astype(jnp.bfloat16))
                spread = spread_kinds(kind, jnp.concatenate(picked, axis=0), kinds_total)
                there = pl.ds(pl.multiple_of((c - first) * size, size), size)
                outs[i][there, :] = jnp.dot(
                    spread, weight_ref[...], preferred_element_type=jnp.float32
                ).astype(jnp.bfloat16)
                part = lax.dot_general(
                    feats_ref[pl.ds(pl.multiple_of(c * size, size), size), :],
                    spread,
                    (((0,), (0,)), ((), ())),
                    preferred_element_type=jnp.float32,
                )
                for k in range(kinds_total):
                    terms_ref[k] += part[:, k * chan_out : (k + 1) * chan_out]

            pl.when(slow)(lambda: work(True))
            pl.when(jnp.logical_not(slow))(lambda: work(False))
            return carry

        lax.fori_loop(first, last, chunk, 0)
    if shares:
        per = kinds_total // shares
        for m in range(shares):
            owner = table_ref[offset + blocks + m]
            rest[m][...] = terms_ref[pl.ds(owner * per, per)].reshape(rest[m].shape)


def stage(table, offset, ends, parents, codes, feats, weight_tall, cots, priors, shares, rows):
    blocks = len(cots)
    chan_out = cots[0].shape[1]
    chan_in = feats.shape[1]
    kinds_total = weight_tall.shape[0] // chan_out
    smem = pl.BlockSpec(memory_space=pltpu.SMEM)
    vmem = pl.BlockSpec(memory_space=pltpu.VMEM)
    args = (table, ends, parents, codes, feats, weight_tall, *cots, *priors)
    outs = [jax.ShapeDtypeStruct((rows, chan_in), jnp.bfloat16)] * blocks
    scratch = []
    terms_shape = (kinds_total, chan_in, chan_out)
    if shares:
        outs += [jax.ShapeDtypeStruct((kinds_total * chan_in // shares, chan_out), jnp.float32)] * shares
        scratch = [pltpu.VMEM(terms_shape, jnp.float32)]
    else:
        outs += [jax.ShapeDtypeStruct(terms_shape, jnp.float32)]
    return pl.pallas_call(
        lambda *refs: stage_kernel(blocks, len(priors), shares, offset, *refs),
        out_shape=outs,
        in_specs=[smem, smem] + [vmem] * (len(args) - 2),
        out_specs=[vmem] * len(outs),
        scratch_shapes=scratch,
        compiler_params=pltpu.CompilerParams(vmem_limit_bytes=VMEM_LIMIT),
        name="fine_gradients",
    )(*args)


def merge_kernel(spans, offset, table_ref, parent_ref, *rest):
    out_ref = rest[-1]
    size = 2 * TILE
    out_ref[...] = jnp.zeros(out_ref.shape, out_ref.dtype)
    parents = parent_ref[...]
    for i, span in enumerate(spans):
        base = table_ref[offset + i]
        first = jnp.sum((parents < base).astype(jnp.int32)) // size
        last = (jnp.sum((parents < base + span).astype(jnp.int32)) + size - 1) // size

        def chunk(c, carry):
            here = pl.ds(pl.multiple_of(c * size, size), size)
            there = pl.ds(pl.multiple_of((c - first) * size, size), size)
            out_ref[here, :] = (
                out_ref[here, :].astype(jnp.float32) + rest[i][there, :].astype(jnp.float32)
            ).astype(out_ref.dtype)
            return carry

        lax.fori_loop(first, last, chunk, 0)


def merge(table, offset, parents, spans, parts, shape):
    vmem = pl.BlockSpec(memory_space=pltpu.VMEM)
    return pl.pallas_call(
        lambda *refs: merge_kernel(spans, offset, *refs),
        out_shape=jax.ShapeDtypeStruct(shape, jnp.bfloat16),
        in_specs=[pl.BlockSpec(memory_space=pltpu.SMEM)] + [vmem] * (1 + len(parts)),
        out_specs=vmem,
        compiler_params=pltpu.CompilerParams(vmem_limit_bytes=VMEM_LIMIT),
        name="merge_gradients",
    )(table, parents, *parts)

GATE_EARLY = 3
LAST = ("up", "dp", 1)


def after(value, *marks):
    return lax.optimization_barrier((value, *marks))[0]


def swap(value, mask, axis):
    size = lax.axis_size(axis)
    return lax.ppermute(value, axis, [(i, i ^ mask) for i in range(size)])


def pick(parts, index):
    return lax.dynamic_index_in_dim(parts, index, 0, keepdims=False)


def sum_terms(keep, send, mark):
    space_size = lax.axis_size("space")
    dp_size = lax.axis_size("dp")
    total = keep + swap(send, 1, "dp")
    trail = [("dp", 1)]
    steps = [("dp", 1 << b) for b in range(1, dp_size.bit_length() - 1)] + [("space", 1)]
    for axis, bit in steps:
        total = mark(("down", axis, bit), total)
        mine = lax.axis_index(axis) // bit % 2
        parts = total.reshape(2, total.shape[0] // 2, total.shape[1])
        total = pick(parts, mine) + swap(pick(parts, 1 - mine), bit, axis)
        trail.append((axis, bit))
    total = mark("across", total)
    if space_size == 8:
        total = (total + swap(total, 2, "space")) + (swap(total, 4, "space") + swap(total, 6, "space"))
    else:
        bit = 2
        while bit < space_size:
            total = total + swap(total, bit, "space")
            bit *= 2
    spot = lax.axis_index("dp") // 2 * 2 + lax.axis_index("space") % 2
    if dp_size == 4:
        total = mark("up", total)
        pairs = [(d * space_size + s, (d ^ 2) * space_size + (s ^ 1)) for d in range(4) for s in range(space_size)]
        by = [total, swap(total, 1, "space"), swap(total, 2, "dp"), lax.ppermute(total, ("dp", "space"), pairs)]
        wide = []
        for place in range(4):
            piece = by[0]
            for k in range(1, 4):
                piece = jnp.where(spot ^ k == place, by[k], piece)
            wide.append(piece)
        total = jnp.concatenate(wide, axis=0)
        trail = trail[:1]
    for axis, bit in trail[::-1]:
        total = mark(("up", axis, bit), total)
        mine = lax.axis_index(axis) // bit % 2
        other = swap(total, bit, axis)
        total = jnp.where(
            mine == 0, jnp.concatenate([total, other]), jnp.concatenate([other, total])
        )
    return total


def table_row(place, bit, cycle, par_rows):
    size = len(cycle)
    spot = cycle.index(place)
    row = [place * par_rows]
    for step in range(1, size // 2):
        row += [cycle[(spot - step) % size] * par_rows, cycle[(spot + step) % size] * par_rows]
    far = cycle[(spot + size // 2) % size] * par_rows
    return row + [far, far + par_rows // 2, bit, 1 - bit]


def per_device(features, child_parent, child_code, weight, out_grad):
    fine_rows = features[0]
    row_count = fine_rows.shape[0]
    parents = child_parent[0].reshape(row_count // LANES, LANES)
    codes = child_code[0].reshape(row_count // LANES, LANES)
    cotangent = out_grad[0]
    par_rows = cotangent.shape[0]
    kinds_total, chan_in, chan_out = weight.shape
    space_size = lax.axis_size("space")
    dp_size = lax.axis_size("dp")
    me = lax.axis_index("space")
    capacity = 2 * row_count // space_size
    weight_flat = weight.reshape(kinds_total * chan_in, chan_out)
    weight_tall = jnp.transpose(weight, (0, 2, 1)).reshape(kinds_total * chan_out, chan_in)
    steps = space_size // 2
    half = par_rows // 2
    cycle = list(range(0, space_size, 2)) + list(range(space_size - 1, 0, -2))
    ahead = [(cycle[i], cycle[(i + 1) % space_size]) for i in range(space_size)]
    behind = [(b, a) for a, b in ahead]
    dp_bit = lax.axis_index("dp") % 2
    table = jnp.asarray(
        [table_row(d, b, cycle, par_rows) for d in range(space_size) for b in range(2)], jnp.int32
    )
    table = lax.dynamic_index_in_dim(table, 2 * me + dp_bit, 0, keepdims=False)
    early, late = pack(parents, codes, fine_rows, space_size, capacity // 2, par_rows)

    tiles = child_parent[0].reshape(row_count // TILE, TILE)
    ends = jnp.stack([tiles[:, 0], tiles[:, TILE - 1]])
    size = 2 * TILE
    window_rows = (-(-(2 * row_count // space_size) // size) + 1) * size
    grads, spans, terms_parts = [], [], []

    def advance(step, blocks, shares=0):
        *parts, = stage(
            table, max(2 * step - 1, 0), ends, parents, codes, fine_rows, weight_tall, blocks,
            terms_parts if shares else (), shares, window_rows,
        )
        grads.extend(parts[: len(blocks)])
        spans.extend(block.shape[0] for block in blocks)
        return parts[len(blocks) :]

    def exchange(windows, mark):
        return lax.all_to_all(after(windows, mark), "space", 0, 0, tiled=True)

    right = left = cotangent
    blocks = (cotangent,)
    for step in range(1, steps + 1):
        if step == steps:
            right, left = right[:half], left[half:]
        right = lax.ppermute(right, "space", ahead)
        left = lax.ppermute(left, "space", behind)
        terms_parts += advance(step - 1, blocks)
        blocks = (right, left)
        if step < steps:
            right, left = lax.optimization_barrier((right, left, terms_parts[-1]))[:2]
        if step == GATE_EARLY:
            early = exchange(early, right)
    blocks = (blocks[0], after(blocks[1], terms_parts[-1]))
    keep, give = advance(steps, blocks, 2)
    late = lax.all_to_all(after(late, *blocks), "space", 0, 0, tiled=True)
    placed = place_children(after(early, keep), weight_flat, None, par_rows, False)
    acc = place_children(late, weight_flat, placed, par_rows, True)

    feature_grad = merge(table, 0, parents, spans, grads, fine_rows.shape)

    def mark(name, value):
        if name == ("down", "dp", 2):
            return after(value, placed)
        if name == LAST:
            return after(value, acc)
        return after(value, feature_grad) if name == "across" else value

    terms = sum_terms(keep, give, mark)
    total_rows = row_count * space_size * dp_size
    summed = terms.reshape(kinds_total, chan_in, chan_out)
    weight_grad = summed / jnp.sqrt(jnp.float32(total_rows))
    return (acc[None], feature_grad[None], weight_grad)


def solution(mesh):
    placed = (
        P("dp", "space", None),
        P("dp", "space"),
        P("dp", "space"),
        P(),
        P("dp", "space", None),
    )
    return jax.shard_map(
        per_device,
        mesh=mesh,
        in_specs=placed,
        out_specs=(P("dp", "space", None), P("dp", "space", None), P()),
        check_vma=False,
    )
```
